512 devices in a mesh: replica: 64 (over x, y, z_lo), tensor: 8 (over z_hi, core).
Axes of the slice: x: 4, y: 8, z: 8 (z_hi: 4, z_lo: 2; z = z_hi * 2 + z_lo), core: 2. Of those that a mesh axis runs over, the one named last changes fastest.
Arguments:
- hidden_in: bfloat16 [3, 512, 8192], P(None, 'replica'), may hold values from -6 to 6
- frozen_query_rows: bfloat16 [3, 512, 8192], P(None, 'replica', 'tensor'), may hold values from -144 to 144
- base_key_value: bfloat16 [2, 3, 512, 1024], P(None, None, 'replica', 'tensor'), may hold values from -6 to 6
- cache: bfloat16 [2, 512, 384, 1024], P(None, 'replica', None, 'tensor'), may hold values from -6 to 6
- lengths: int32 [512], P('replica'), may hold values from 2 to 384, as said below
- switch_step: int32 [64], P('replica'), may hold values from 0 to 3
- old_down_q: bfloat16 [64, 8192], replicated, may hold values from -0.0625 to 0.0625
- current_query_up: bfloat16 [64, 8192], P(None, 'tensor'), may hold values from -0.75 to 0.75
- old_down_o: bfloat16 [64, 8192], P(None, 'tensor'), may hold values from -0.0625 to 0.0625
- old_up_o: bfloat16 [64, 8192], replicated, may hold values from -6 to 6
- new_down_q: bfloat16 [64, 8192], P('replica'), may hold values from -0.0625 to 0.0625
- refreshed_query_up: bfloat16 [64, 8192], P('replica', 'tensor'), may hold values from -0.75 to 0.75
- new_down_o: bfloat16 [64, 8192], P('replica', 'tensor'), may hold values from -0.0625 to 0.0625
- new_up_o: bfloat16 [64, 8192], P('replica'), may hold values from -6 to 6
Outputs:
- attended: bfloat16 [3, 512, 8192], P(None, 'replica', 'tensor')
- adapter_out: bfloat16 [3, 512, 8192], P(None, 'replica', 'tensor')
The draws below stay inside these ranges and needn't reach their ends.
Inputs may be any that keep to these rules, and one draw needn't show every extreme that they name: `lengths`: the first sequence of every replica has all 384 positions live.
All inputs are finite; a program needn't handle non-finite values.
Results may differ from the reference program's by a relative error of at most 0.01.
Values may be sent and summed in bfloat16 or wider, within the bound.
A program may use at most 64 MiB of HBM per device.

```python
import jax
import jax.numpy as jnp
from jax import lax

D = 8192
HEADS = 64
KVH = 8
HD = 128
RANK = 64
STEPS = 3
ROWS = 8
CACHE = 384
REPLICAS = 64
BATCH = 512
N_REPLICA = 64


def shared_cache(key):
    return jnp.clip(jax.random.normal(jax.random.fold_in(key, 11), (2, BATCH, CACHE, KVH * HD), jnp.float32), -6.0, 6.0)


def draw_cache(key, part):
    drawn = shared_cache(key)
    return drawn.astype(jnp.bfloat16)


def draw_frozen_query_rows(key, part):
    key = jax.random.fold_in(key, 5)
    drawn = jnp.clip(jax.random.normal(key, (STEPS, BATCH, HEADS * HD), jnp.float32), -6.0, 6.0)
    return drawn.astype(jnp.bfloat16)


def draw_lengths(key, part):
    key = jax.random.fold_in(key, 7)
    drawn = jax.random.randint(key, (BATCH,), 2, CACHE + 1, dtype=jnp.int32)
    row_ids = jnp.arange(BATCH, dtype=jnp.int32)
    return jnp.where(row_ids % ROWS == 0, CACHE, drawn).astype(jnp.int32)


def plant(array, rng, smallest, largest):
    index_at = [jax.random.randint(jax.random.fold_in(rng, axis), (), 0, length) for axis, length in enumerate(array.shape)]
    longest = array.shape.index(max(array.shape))
    beside = index_at[:longest] + [(index_at[longest] + 1) % array.shape[longest]] + index_at[longest + 1:]
    return array.at[tuple(index_at)].set(smallest).at[tuple(beside)].set(largest)


def levels(own_key, shape, shards, smallest, largest):
    level, own = 1.0, jax.random.fold_in(own_key, 6)
    for dim, shards_of in shards:
        draws = jnp.exp(jax.random.uniform(jax.random.fold_in(own, dim), (shards_of,), jnp.float32, smallest / len(shards), largest / len(shards)))
        level = level * jnp.repeat(draws, shape[dim] // shards_of).reshape([-1 if axis == dim else 1 for axis in range(len(shape))])
    return level


def scatter_about(stream_key, extent, deviation, most, shards=(), kind=jnp.bfloat16):
    values = jax.random.normal(stream_key, extent, jnp.float32) * deviation
    if len(shards) > 0:
        values = levels(stream_key, extent, shards, -0.22, 0.18) * values
    return jnp.clip(values, min=-most, max=most).astype(kind)


def setup_inputs(seed: int = 0) -> dict:
    arg_keys = jax.random.split(jax.random.key(seed), 15)
    return {
        "hidden_in": scatter_about(arg_keys[0], (STEPS, BATCH, D), 1.0, 6.0, ((1, 64),)),
        "frozen_query_rows": draw_frozen_query_rows(jax.random.fold_in(arg_keys[14], 71), 0),
        "base_key_value": scatter_about(arg_keys[2], (2, STEPS, BATCH, KVH * HD), 1.0, 6.0, ((2, 64), (3, 8))),
        "cache": draw_cache(jax.random.fold_in(arg_keys[14], 71), 0),
        "lengths": draw_lengths(jax.random.fold_in(arg_keys[14], 71), 0),
        "switch_step": plant(jax.random.randint(arg_keys[5], (REPLICAS,), 0, STEPS + 1), jax.random.fold_in(arg_keys[5], 1), 0, STEPS).astype(jnp.int32),
        "old_down_q": scatter_about(arg_keys[6], (RANK, D), D ** -0.5, 0.0625),
        "current_query_up": scatter_about(arg_keys[7], (RANK, HEADS * HD), RANK ** -0.5, 0.75, ((1, 8),)),
        "old_down_o": scatter_about(arg_keys[8], (RANK, HEADS * HD), (HEADS * HD) ** -0.5, 0.0625, ((1, 8),)),
        "old_up_o": scatter_about(arg_keys[9], (RANK, D), 1.0, 6.0),
        "new_down_q": scatter_about(arg_keys[10], (RANK, D), D ** -0.5, 0.0625, ((0, 64),)),
        "refreshed_query_up": scatter_about(arg_keys[11], (RANK, HEADS * HD), RANK ** -0.5, 0.75, ((0, 64), (1, 8))),
        "new_down_o": scatter_about(arg_keys[12], (RANK, HEADS * HD), (HEADS * HD) ** -0.5, 0.0625, ((0, 64), (1, 8))),
        "new_up_o": scatter_about(arg_keys[13], (RANK, D), 1.0, 6.0, ((0, 64),)),
    }


def attend(query_matrix, cache_keys, cache_values, fresh_keys, fresh_values, lengths):
    score_scale = 1.0 / (query_matrix.shape[-1] ** 0.5)
    q32 = query_matrix.astype(jnp.float32)
    cache_scores = jnp.einsum('bkgd,blkd->bkgl', q32, cache_keys.astype(jnp.float32)) * score_scale
    positions = jnp.arange(cache_keys.shape[1], dtype=jnp.int32)
    visible = (positions[None, :] < lengths[:, None])[:, None, None, :]
    cache_scores = jnp.where(visible, cache_scores, jnp.float32(-1e30))
    fresh_scores = jnp.einsum('bkgd,bukd->bkgu', q32, fresh_keys.astype(jnp.float32)) * score_scale
    row_max = jnp.maximum(jnp.max(cache_scores, axis=-1), jnp.max(fresh_scores, axis=-1))[..., None]
    cache_exp = jnp.exp(cache_scores - row_max)
    fresh_exp = jnp.exp(fresh_scores - row_max)
    row_total = jnp.sum(cache_exp, axis=-1, keepdims=True) + jnp.sum(fresh_exp, axis=-1, keepdims=True)
    cache_weights = (cache_exp / row_total).astype(jnp.bfloat16)
    fresh_weights = (fresh_exp / row_total).astype(jnp.bfloat16)
    result = jnp.einsum('bkgl,blkd->bkgd', cache_weights.astype(jnp.float32), cache_values.astype(jnp.float32))
    result = result + jnp.einsum('bkgu,bukd->bkgd', fresh_weights.astype(jnp.float32), fresh_values.astype(jnp.float32))
    return result.astype(jnp.bfloat16)


def reference(hidden_in, frozen_query_rows, base_key_value, cache, lengths, switch_step, old_down_q, current_query_up, old_down_o, old_up_o, new_down_q, refreshed_query_up, new_down_o, new_up_o):
    groups = HEADS // KVH
    row_switch = jnp.repeat(switch_step, ROWS)
    cache_keys = cache[0].reshape(N_REPLICA, ROWS, CACHE, KVH, HD)
    cache_values = cache[1].reshape(N_REPLICA, ROWS, CACHE, KVH, HD)
    fresh_keys = jnp.transpose(base_key_value[0], (1, 0, 2)).reshape(N_REPLICA, ROWS, STEPS, KVH, HD)
    fresh_values = jnp.transpose(base_key_value[1], (1, 0, 2)).reshape(N_REPLICA, ROWS, STEPS, KVH, HD)
    block_lengths = lengths.reshape(N_REPLICA, ROWS)
    attended_list = []
    adapter_list = []
    for decode_step in range(STEPS):
        adapter_swapped = (decode_step >= row_switch)[:, None]
        inputs = hidden_in[decode_step]
        current_rank_part = jnp.dot(inputs, old_down_q.T, preferred_element_type=jnp.float32).astype(jnp.bfloat16)
        refreshed_rank_part = jnp.dot(inputs, new_down_q.T, preferred_element_type=jnp.float32).astype(jnp.bfloat16)
        adapter_query_delta = jnp.where(adapter_swapped, jnp.dot(refreshed_rank_part, refreshed_query_up, preferred_element_type=jnp.float32), jnp.dot(current_rank_part, current_query_up, preferred_element_type=jnp.float32))
        query_matrix = (frozen_query_rows[decode_step].astype(jnp.float32) + adapter_query_delta).astype(jnp.bfloat16)
        query_matrix = query_matrix.reshape(N_REPLICA, ROWS, KVH, groups, HD)

        def block_attend(pieces):
            return attend(pieces[0], pieces[1], pieces[2], pieces[3], pieces[4], pieces[5])

        attended = lax.map(block_attend, (query_matrix, cache_keys, cache_values, fresh_keys[:, :, :decode_step + 1], fresh_values[:, :, :decode_step + 1], block_lengths))
        attended = attended.reshape(BATCH, HEADS * HD)
        rank_old = jnp.dot(attended, old_down_o.T, preferred_element_type=jnp.float32)
        rank_new = jnp.dot(attended, new_down_o.T, preferred_element_type=jnp.float32)
        rank_sum = jnp.where(adapter_swapped, rank_new, rank_old).astype(jnp.bfloat16)
        adapter = jnp.where(adapter_swapped, jnp.dot(rank_sum, new_up_o, preferred_element_type=jnp.float32), jnp.dot(rank_sum, old_up_o, preferred_element_type=jnp.float32))
        attended_list.append(attended)
        adapter_list.append(adapter.astype(jnp.bfloat16))
    return jnp.stack(attended_list), jnp.stack(adapter_list)
```

```python
import functools

import jax
import jax.numpy as jnp
from jax import lax
from jax.experimental import pallas as pl
from jax.experimental.pallas import tpu as pltpu
from jax.sharding import PartitionSpec as P

HD = 128
STEPS = 3
ROWS = 8
RANK = 64
GROUP = 16
LANES = 128
MESH = pl.DeviceIdType.MESH
F32 = jnp.float32
BF16 = jnp.bfloat16


def nt(a, b):
    return lax.dot_general(a, b, (((1,), (1,)), ((), ())), preferred_element_type=F32)


def nn(a, b):
    return lax.dot_general(a, b, (((1,), (0,)), ((), ())), preferred_element_type=F32)


def kernel(
    n_block, n_tensor, width, cache_len, key_rows,
    lengths, switch, hidden, frozen, fresh, cache,
    old_dq, old_uq, old_do, old_uo, new_dq, new_uq, new_do, new_uo,
    attended_out, adapter_out,
    row_dq, row_uq, row_do, row_uo, hid, frz, frs, kbuf, vbuf,
    w_old, w_new, packs, landed, stage, spread, fresh_rows, q_heads, a_rows,
    part, parts, att_stage, ada_stage,
    loc, kv_sem, s1_send, s1_recv, s2_send, s2_recv, ar_send, ar_recv,
):
    replica = lax.axis_index("replica")
    tensor = lax.axis_index("tensor")
    mine = lax.rem(replica, GROUP)
    block = lax.div(replica, GROUP)
    base = block * GROUP
    cols = pl.ds(pl.multiple_of(tensor * width, width), width)
    heads = width // HD
    tiles = width // LANES

    local = [
        pltpu.make_async_copy(new_dq, row_dq, loc.at[0]),
        pltpu.make_async_copy(new_uq, row_uq, loc.at[1]),
        pltpu.make_async_copy(new_do, row_do, loc.at[2]),
        pltpu.make_async_copy(new_uo, row_uo, loc.at[3]),
        pltpu.make_async_copy(hidden.at[:, :, cols], hid, loc.at[4]),
        pltpu.make_async_copy(old_dq.at[:, cols], w_old.at[0], loc.at[5]),
        pltpu.make_async_copy(fresh, frs, loc.at[6]),
        pltpu.make_async_copy(old_uq, w_old.at[1], loc.at[7]),
        pltpu.make_async_copy(frozen, frz, loc.at[8]),
        pltpu.make_async_copy(old_do, w_old.at[2], loc.at[9]),
        pltpu.make_async_copy(old_uo.at[:, cols], w_old.at[3], loc.at[10]),
    ]
    for copy in local:
        copy.start()
    kv = []
    for b in range(ROWS):
        kv.append(pltpu.make_async_copy(cache.at[0, b], kbuf.at[b, pl.ds(0, cache_len)], kv_sem.at[0, b]))
        kv.append(pltpu.make_async_copy(cache.at[1, b], vbuf.at[b, pl.ds(0, cache_len)], kv_sem.at[1, b]))
    for copy in kv:
        copy.start()

    group_peers = [(base + lax.rem(mine + j, GROUP), tensor) for j in range(1, GROUP)]
    block_peers = [
        (lax.rem(block + j, n_block) * GROUP + mine, tensor) for j in range(1, n_block)
    ]
    tensor_peers = [(replica, lax.rem(tensor + j, n_tensor)) for j in range(1, n_tensor)]
    barrier = pltpu.get_barrier_semaphore()
    everyone = group_peers + block_peers + tensor_peers
    for peer in everyone:
        pl.semaphore_signal(barrier, inc=1, device_id=peer, device_id_type=MESH)

    for copy in local[:4]:
        copy.wait()
    for i, row in enumerate((row_dq[:, cols], row_uq[...], row_do[...], row_uo[:, cols])):
        row = row.astype(F32)
        for s in range(tiles):
            stage[i // 2, pl.ds((i % 2) * tiles + s, 1), :] = row[:, s * LANES : (s + 1) * LANES]
    for p in range(2):
        packs[p] = stage[p].astype(BF16)
        landed[p, mine] = packs[p]

    pl.semaphore_wait(barrier, len(everyone))

    for p in range(2):
        for peer in group_peers:
            pltpu.make_async_remote_copy(
                src_ref=packs.at[p],
                dst_ref=landed.at[p, mine],
                send_sem=s1_send.at[p],
                recv_sem=s1_recv.at[p],
                device_id=peer,
                device_id_type=MESH,
            ).start()

    local[6].wait()
    pad = key_rows - cache_len - 16
    for i, buf in enumerate((kbuf, vbuf)):
        for u in range(ROWS):
            if u < STEPS:
                fresh_rows[i, pl.ds(u * ROWS, ROWS), :] = frs[i, u].astype(F32)
            else:
                fresh_rows[i, pl.ds(u * ROWS, ROWS), :] = jnp.zeros((ROWS, HD), F32)
        for b in range(ROWS):
            rows = fresh_rows[i, pl.ds(b, ROWS, stride=ROWS), :]
            rows = jnp.concatenate([rows, jnp.zeros((8, HD), F32)], axis=0)
            buf[b, pl.ds(cache_len, 16), :] = rows.astype(BF16)
            buf[b, pl.ds(cache_len + 16, pad), :] = jnp.zeros((pad, HD), BF16)

    local[4].wait()
    hid_rows = jnp.concatenate([hid[t].astype(F32) for t in range(STEPS)], axis=0).astype(BF16)

    own_rows = pl.ds(pl.multiple_of(block * GROUP, GROUP), GROUP)

    def gathered(p):
        pltpu.make_async_copy(
            landed.at[p, pl.ds(0, GROUP - 1)], landed.at[p, pl.ds(0, GROUP - 1)], s1_recv.at[p]
        ).wait()
        spread[...] = landed[p].reshape(GROUP * 2 * tiles, LANES).astype(F32)
        for half in range(2):
            m = 2 * p + half
            for s in range(tiles):
                w_new[m, own_rows, s * LANES : (s + 1) * LANES] = spread[
                    pl.ds(half * tiles + s, GROUP, stride=2 * tiles), :
                ].astype(BF16)
            for peer in block_peers:
                pltpu.make_async_remote_copy(
                    src_ref=w_new.at[m, own_rows],
                    dst_ref=w_new.at[m, own_rows],
                    send_sem=s2_send.at[m],
                    recv_sem=s2_recv.at[m],
                    device_id=peer,
                    device_id_type=MESH,
                ).start()

    def weights(m):
        others = w_new.at[m, pl.ds(0, (n_block - 1) * GROUP)]
        pltpu.make_async_copy(others, others, s2_recv.at[m]).wait()
        return jnp.concatenate([w_old[m], w_new[m]], axis=0)

    lane_half = lax.div(lax.broadcasted_iota(jnp.int32, (ROWS, LANES), 1), RANK)
    switch_at = jnp.full((ROWS, LANES), switch[0], jnp.int32)
    half_of = [jnp.where(switch_at <= t, 1, 0) for t in range(STEPS)]

    def reduce_start(r, product):
        chosen = []
        for t in range(STEPS):
            rows = product[t * ROWS : (t + 1) * ROWS]
            chosen.append(jnp.where(half_of[t] == t % 2, rows, pltpu.roll(rows, RANK, 1)))
        tile = jnp.concatenate([jnp.where(lane_half == 0, chosen[0], chosen[1]), chosen[2]], axis=0)
        part[r] = tile
        parts[r, tensor] = tile
        for peer in tensor_peers:
            pltpu.make_async_remote_copy(
                src_ref=part.at[r],
                dst_ref=parts.at[r, tensor],
                send_sem=ar_send.at[r],
                recv_sem=ar_recv.at[r],
                device_id=peer,
                device_id_type=MESH,
            ).start()

    def reduce_done(r):
        others = parts.at[r, pl.ds(0, n_tensor - 1)]
        pltpu.make_async_copy(others, others, ar_recv.at[r]).wait()
        total = jnp.sum(parts[r], axis=0)
        rows = []
        for t in range(STEPS):
            tile = total[(t // 2) * ROWS : (t // 2 + 1) * ROWS]
            both = jnp.where(lane_half == t % 2, tile, pltpu.roll(tile, RANK, 1))
            rows.append(jnp.where(lane_half == half_of[t], both, 0.0))
        return jnp.concatenate(rows, axis=0).astype(BF16)

    gathered(0)
    gathered(1)

    local[5].wait()
    reduce_start(0, nt(hid_rows, weights(0)))

    local[7].wait()
    local[8].wait()
    up_q = weights(1)
    for copy in kv:
        copy.wait()
    low_rank = reduce_done(0)
    delta = nn(low_rank, up_q)
    for t in range(STEPS):
        for h in range(heads):
            at = slice(h * HD, (h + 1) * HD)
            q_heads[t, pl.ds(h * ROWS, ROWS), :] = (
                frz[t, :, at].astype(F32) + delta[t * ROWS : (t + 1) * ROWS, at]
            )

    scale = 1.0 / HD**0.5
    query_rows = STEPS * heads
    col = lax.broadcasted_iota(jnp.int32, (query_rows, key_rows), 1)
    row = lax.broadcasted_iota(jnp.int32, (query_rows, key_rows), 0)
    is_fresh = jnp.logical_and(col >= cache_len, (col - cache_len) * heads <= row)
    for b in range(ROWS):
        query = jnp.concatenate(
            [q_heads[t, pl.ds(b, heads, stride=ROWS), :] for t in range(STEPS)], axis=0
        ).astype(BF16)
        scores = nt(query, kbuf[b]) * scale
        live = jnp.logical_or(col < lengths[b], is_fresh)
        scores = jnp.where(live, scores, -1e30)
        top = jnp.max(scores, axis=1, keepdims=True)
        exps = jnp.exp(scores - top)
        total = jnp.sum(exps, axis=1, keepdims=True)
        probs = (exps * (1.0 / total)).astype(BF16)
        result = nn(probs, vbuf[b])
        for t in range(STEPS):
            a_rows[t, pl.ds(b * heads, heads), :] = result[t * heads : (t + 1) * heads]

    attended = []
    for t in range(STEPS):
        rows = jnp.concatenate(
            [a_rows[t, pl.ds(h, ROWS, stride=heads), :] for h in range(heads)], axis=1
        )
        attended.append(rows)
        att_stage[t] = rows.astype(BF16)
    att_copy = pltpu.make_async_copy(att_stage, attended_out, loc.at[11])
    att_copy.start()

    local[9].wait()
    reduce_start(1, nt(jnp.concatenate(attended, axis=0).astype(BF16), weights(2)))
    local[10].wait()
    up_o = weights(3)
    result = nn(reduce_done(1), up_o)
    for t in range(STEPS):
        ada_stage[t] = result[t * ROWS : (t + 1) * ROWS].astype(BF16)
    ada_copy = pltpu.make_async_copy(ada_stage, adapter_out, loc.at[12])
    ada_copy.start()

    for p in range(2):
        sent = landed.at[p, pl.ds(0, GROUP - 1)]
        pltpu.make_async_copy(sent, sent, s1_send.at[p]).wait()
    for m in range(4):
        sent = w_new.at[m, pl.ds(0, (n_block - 1) * GROUP)]
        pltpu.make_async_copy(sent, sent, s2_send.at[m]).wait()
    for r in range(2):
        sent = parts.at[r, pl.ds(0, n_tensor - 1)]
        pltpu.make_async_copy(sent, sent, ar_send.at[r]).wait()
    att_copy.wait()
    ada_copy.wait()


def body(
    n_replica, n_tensor,
    hidden_in, frozen_query_rows, base_key_value, cache, lengths, switch_step,
    old_down_q, current_query_up, old_down_o, old_up_o,
    new_down_q, refreshed_query_up, new_down_o, new_up_o,
):
    width = frozen_query_rows.shape[-1]
    cache_len = cache.shape[2]
    key_rows = cache_len + LANES
    tiles = width // LANES
    dma = pltpu.SemaphoreType.DMA
    out = jax.ShapeDtypeStruct(frozen_query_rows.shape, BF16)
    return pl.pallas_call(
        functools.partial(kernel, n_replica // GROUP, n_tensor, width, cache_len, key_rows),
        out_shape=(out, out),
        in_specs=[pl.BlockSpec(memory_space=pltpu.SMEM)] * 2
        + [pl.BlockSpec(memory_space=pl.ANY)] * 12,
        out_specs=(pl.BlockSpec(memory_space=pl.ANY),) * 2,
        scratch_shapes=[
            pltpu.VMEM(new_down_q.shape, BF16),
            pltpu.VMEM(refreshed_query_up.shape, BF16),
            pltpu.VMEM(new_down_o.shape, BF16),
            pltpu.VMEM(new_up_o.shape, BF16),
            pltpu.VMEM((STEPS, ROWS, width), BF16),
            pltpu.VMEM((STEPS, ROWS, width), BF16),
            pltpu.VMEM(base_key_value.shape, BF16),
            pltpu.VMEM((ROWS, key_rows, HD), BF16),
            pltpu.VMEM((ROWS, key_rows, HD), BF16),
            pltpu.VMEM((4, RANK, width), BF16),
            pltpu.VMEM((4, RANK, width), BF16),
            pltpu.VMEM((2, 2 * tiles, LANES), BF16),
            pltpu.VMEM((2, GROUP, 2 * tiles, LANES), BF16),
            pltpu.VMEM((2, 2 * tiles, LANES), F32),
            pltpu.VMEM((GROUP * 2 * tiles, LANES), F32),
            pltpu.VMEM((2, ROWS * ROWS, HD), F32),
            pltpu.VMEM((STEPS, width // HD * ROWS, HD), F32),
            pltpu.VMEM((STEPS, width // HD * ROWS, HD), F32),
            pltpu.VMEM((2, 2 * ROWS, LANES), F32),
            pltpu.VMEM((2, n_tensor, 2 * ROWS, LANES), F32),
            pltpu.VMEM((STEPS, ROWS, width), BF16),
            pltpu.VMEM((STEPS, ROWS, width), BF16),
            dma((13,)),
            dma((2, ROWS)),
            dma((2,)),
            dma((2,)),
            dma((4,)),
            dma((4,)),
            dma((2,)),
            dma((2,)),
        ],
        compiler_params=pltpu.CompilerParams(
            collective_id=0, has_side_effects=True, vmem_limit_bytes=32 * 1024 * 1024
        ),
    )(
        lengths, switch_step, hidden_in, frozen_query_rows, base_key_value, cache,
        old_down_q, current_query_up, old_down_o, old_up_o,
        new_down_q, refreshed_query_up, new_down_o, new_up_o,
    )


def solution(mesh):
    placed = (
        P(None, "replica", None),
        P(None, "replica", "tensor"),
        P(None, None, "replica", "tensor"),
        P(None, "replica", None, "tensor"),
        P("replica"),
        P("replica"),
        P(),
        P(None, "tensor"),
        P(None, "tensor"),
        P(),
        P("replica", None),
        P("replica", "tensor"),
        P("replica", "tensor"),
        P("replica", None),
    )
    return jax.shard_map(
        functools.partial(body, mesh.shape["replica"], mesh.shape["tensor"]),
        mesh=mesh,
        in_specs=placed,
        out_specs=(P(None, "replica", "tensor"), P(None, "replica", "tensor")),
        check_vma=False,
    )
```

```python
import functools

import jax
import jax.numpy as jnp
from jax import lax
from jax.experimental import pallas as pl
from jax.experimental.pallas import tpu as pltpu
from jax.sharding import PartitionSpec as P

HD = 128
STEPS = 3
ROWS = 8
RANK = 64
GROUP = 16
LANES = 128
MESH = pl.DeviceIdType.MESH
F32 = jnp.float32
BF16 = jnp.bfloat16


def nt(a, b):
    return lax.dot_general(a, b, (((1,), (1,)), ((), ())), preferred_element_type=F32)


def nn(a, b):
    return lax.dot_general(a, b, (((1,), (0,)), ((), ())), preferred_element_type=F32)


def kernel(
    n_block, n_tensor, width, cache_len, key_rows,
    switch, lengths_in, hidden, frozen, fresh, cache,
    old_dq, old_uq, old_do, old_uo, new_dq, new_uq, new_do, new_uo,
    attended_out, adapter_out,
    row_dq, row_uq, row_do, row_uo, hid, frz, frs, kbuf, vbuf,
    w_old, w_new, packs, landed, stage, spread, fresh_rows, q_heads, a_rows,
    part, parts, att_stage, ada_stage, lengths,
    loc, kv_sem, s1_send, s1_recv, s2_send, s2_recv, ar_send, ar_recv,
):
    replica = lax.axis_index("replica")
    tensor = lax.axis_index("tensor")
    mine = lax.rem(replica, GROUP)
    block = lax.div(replica, GROUP)
    base = block * GROUP
    cols = pl.ds(pl.multiple_of(tensor * width, width), width)
    heads = width // HD
    tiles = width // LANES

    local = [
        pltpu.make_async_copy(new_dq, row_dq, loc.at[0]),
        pltpu.make_async_copy(new_uq, row_uq, loc.at[1]),
        pltpu.make_async_copy(new_do, row_do, loc.at[2]),
        pltpu.make_async_copy(new_uo, row_uo, loc.at[3]),
        pltpu.make_async_copy(hidden.at[:, :, cols], hid, loc.at[4]),
        pltpu.make_async_copy(old_dq.at[:, cols], w_old.at[0], loc.at[5]),
        pltpu.make_async_copy(fresh, frs, loc.at[6]),
        pltpu.make_async_copy(old_uq, w_old.at[1], loc.at[7]),
        pltpu.make_async_copy(frozen, frz, loc.at[8]),
        pltpu.make_async_copy(old_do, w_old.at[2], loc.at[9]),
        pltpu.make_async_copy(old_uo.at[:, cols], w_old.at[3], loc.at[10]),
        pltpu.make_async_copy(lengths_in, lengths, loc.at[13]),
    ]
    for copy in local:
        copy.start()
    kv = []
    for b in range(ROWS):
        kv.append(pltpu.make_async_copy(cache.at[0, b], kbuf.at[b, pl.ds(0, cache_len)], kv_sem.at[0, b]))
        kv.append(pltpu.make_async_copy(cache.at[1, b], vbuf.at[b, pl.ds(0, cache_len)], kv_sem.at[1, b]))
    for copy in kv:
        copy.start()

    group_peers = [(base + lax.rem(mine + j, GROUP), tensor) for j in range(1, GROUP)]
    block_peers = [
        (lax.rem(block + j, n_block) * GROUP + mine, tensor) for j in range(1, n_block)
    ]
    tensor_peers = [(replica, lax.rem(tensor + j, n_tensor)) for j in range(1, n_tensor)]
    barrier = pltpu.get_barrier_semaphore()
    everyone = group_peers + block_peers + tensor_peers
    for peer in everyone:
        pl.semaphore_signal(barrier, inc=1, device_id=peer, device_id_type=MESH)

    for copy in local[:4]:
        copy.wait()
    for i, row in enumerate((row_dq[:, cols], row_uq[...], row_do[...], row_uo[:, cols])):
        row = row.astype(F32)
        for s in range(tiles):
            stage[i // 2, pl.ds((i % 2) * tiles + s, 1), :] = row[:, s * LANES : (s + 1) * LANES]
    for p in range(2):
        packs[p] = stage[p].astype(BF16)
        landed[p, mine] = packs[p]

    pl.semaphore_wait(barrier, len(everyone))

    for p in range(2):
        for peer in group_peers:
            pltpu.make_async_remote_copy(
                src_ref=packs.at[p],
                dst_ref=landed.at[p, mine],
                send_sem=s1_send.at[p],
                recv_sem=s1_recv.at[p],
                device_id=peer,
                device_id_type=MESH,
            ).start()

    local[6].wait()
    pad = key_rows - cache_len - 16
    for i, buf in enumerate((kbuf, vbuf)):
        for u in range(ROWS):
            if u < STEPS:
                fresh_rows[i, pl.ds(u * ROWS, ROWS), :] = frs[i, u].astype(F32)
            else:
                fresh_rows[i, pl.ds(u * ROWS, ROWS), :] = jnp.zeros((ROWS, HD), F32)
        for b in range(ROWS):
            rows = fresh_rows[i, pl.ds(b, ROWS, stride=ROWS), :]
            rows = jnp.concatenate([rows, jnp.zeros((8, HD), F32)], axis=0)
            buf[b, pl.ds(cache_len, 16), :] = rows.astype(BF16)
            buf[b, pl.ds(cache_len + 16, pad), :] = jnp.zeros((pad, HD), BF16)

    local[4].wait()
    hid_rows = jnp.concatenate([hid[t].astype(F32) for t in range(STEPS)], axis=0).astype(BF16)

    own_rows = pl.ds(pl.multiple_of(block * GROUP, GROUP), GROUP)

    def gathered(p):
        pltpu.make_async_copy(
            landed.at[p, pl.ds(0, GROUP - 1)], landed.at[p, pl.ds(0, GROUP - 1)], s1_recv.at[p]
        ).wait()
        spread[...] = landed[p].reshape(GROUP * 2 * tiles, LANES).astype(F32)
        for half in range(2):
            m = 2 * p + half
            for s in range(tiles):
                w_new[m, own_rows, s * LANES : (s + 1) * LANES] = spread[
                    pl.ds(half * tiles + s, GROUP, stride=2 * tiles), :
                ].astype(BF16)
            for peer in block_peers:
                pltpu.make_async_remote_copy(
                    src_ref=w_new.at[m, own_rows],
                    dst_ref=w_new.at[m, own_rows],
                    send_sem=s2_send.at[m],
                    recv_sem=s2_recv.at[m],
                    device_id=peer,
                    device_id_type=MESH,
                ).start()

    def weights(m):
        others = w_new.at[m, pl.ds(0, (n_block - 1) * GROUP)]
        pltpu.make_async_copy(others, others, s2_recv.at[m]).wait()
        return jnp.concatenate([w_old[m], w_new[m]], axis=0)

    lane_half = lax.div(lax.broadcasted_iota(jnp.int32, (ROWS, LANES), 1), RANK)
    switch_at = jnp.full((ROWS, LANES), switch[0], jnp.int32)
    half_of = [jnp.where(switch_at <= t, 1, 0) for t in range(STEPS)]

    def reduce_start(r, product):
        chosen = []
        for t in range(STEPS):
            rows = product[t * ROWS : (t + 1) * ROWS]
            chosen.append(jnp.where(half_of[t] == t % 2, rows, pltpu.roll(rows, RANK, 1)))
        tile = jnp.concatenate([jnp.where(lane_half == 0, chosen[0], chosen[1]), chosen[2]], axis=0)
        part[r] = tile
        parts[r, tensor] = tile
        for peer in tensor_peers:
            pltpu.make_async_remote_copy(
                src_ref=part.at[r],
                dst_ref=parts.at[r, tensor],
                send_sem=ar_send.at[r],
                recv_sem=ar_recv.at[r],
                device_id=peer,
                device_id_type=MESH,
            ).start()

    def reduce_done(r):
        others = parts.at[r, pl.ds(0, n_tensor - 1)]
        pltpu.make_async_copy(others, others, ar_recv.at[r]).wait()
        total = jnp.sum(parts[r], axis=0)
        rows = []
        for t in range(STEPS):
            tile = total[(t // 2) * ROWS : (t // 2 + 1) * ROWS]
            both = jnp.where(lane_half == t % 2, tile, pltpu.roll(tile, RANK, 1))
            rows.append(jnp.where(lane_half == half_of[t], both, 0.0))
        return jnp.concatenate(rows, axis=0).astype(BF16)

    gathered(0)
    gathered(1)

    local[5].wait()
    reduce_start(0, nt(hid_rows, weights(0)))

    local[7].wait()
    local[8].wait()
    up_q = weights(1)
    for copy in kv:
        copy.wait()
    local[11].wait()
    low_rank = reduce_done(0)
    delta = nn(low_rank, up_q)
    for t in range(STEPS):
        for h in range(heads):
            at = slice(h * HD, (h + 1) * HD)
            q_heads[t, pl.ds(h * ROWS, ROWS), :] = (
                frz[t, :, at].astype(F32) + delta[t * ROWS : (t + 1) * ROWS, at]
            )

    scale = 1.0 / HD**0.5
    query_rows = STEPS * heads
    col = lax.broadcasted_iota(jnp.int32, (query_rows, key_rows), 1)
    row = lax.broadcasted_iota(jnp.int32, (query_rows, key_rows), 0)
    is_fresh = jnp.logical_and(col >= cache_len, (col - cache_len) * heads <= row)
    for b in range(ROWS):
        query = jnp.concatenate(
            [q_heads[t, pl.ds(b, heads, stride=ROWS), :] for t in range(STEPS)], axis=0
        ).astype(BF16)
        scores = nt(query, kbuf[b]) * scale
        live = jnp.logical_or(col < lengths[b], is_fresh)
        scores = jnp.where(live, scores, -1e30)
        top = jnp.max(scores, axis=1, keepdims=True)
        exps = jnp.exp(scores - top)
        total = jnp.sum(exps, axis=1, keepdims=True)
        probs = (exps * (1.0 / total)).astype(BF16)
        result = nn(probs, vbuf[b])
        for t in range(STEPS):
            a_rows[t, pl.ds(b * heads, heads), :] = result[t * heads : (t + 1) * heads]

    attended = []
    for t in range(STEPS):
        rows = jnp.concatenate(
            [a_rows[t, pl.ds(h, ROWS, stride=heads), :] for h in range(heads)], axis=1
        )
        attended.append(rows)
        att_stage[t] = rows.astype(BF16)
    att_copy = pltpu.make_async_copy(att_stage, attended_out, loc.at[11])
    att_copy.start()

    local[9].wait()
    reduce_start(1, nt(jnp.concatenate(attended, axis=0).astype(BF16), weights(2)))
    local[10].wait()
    up_o = weights(3)
    result = nn(reduce_done(1), up_o)
    for t in range(STEPS):
        ada_stage[t] = result[t * ROWS : (t + 1) * ROWS].astype(BF16)
    ada_copy = pltpu.make_async_copy(ada_stage, adapter_out, loc.at[12])
    ada_copy.start()

    for p in range(2):
        sent = landed.at[p, pl.ds(0, GROUP - 1)]
        pltpu.make_async_copy(sent, sent, s1_send.at[p]).wait()
    for m in range(4):
        sent = w_new.at[m, pl.ds(0, (n_block - 1) * GROUP)]
        pltpu.make_async_copy(sent, sent, s2_send.at[m]).wait()
    for r in range(2):
        sent = parts.at[r, pl.ds(0, n_tensor - 1)]
        pltpu.make_async_copy(sent, sent, ar_send.at[r]).wait()
    att_copy.wait()
    ada_copy.wait()


def body(
    n_replica, n_tensor,
    hidden_in, frozen_query_rows, base_key_value, cache, lengths, switch_step,
    old_down_q, current_query_up, old_down_o, old_up_o,
    new_down_q, refreshed_query_up, new_down_o, new_up_o,
):
    width = frozen_query_rows.shape[-1]
    cache_len = cache.shape[2]
    key_rows = cache_len + LANES
    tiles = width // LANES
    dma = pltpu.SemaphoreType.DMA
    out = jax.ShapeDtypeStruct(frozen_query_rows.shape, BF16)
    return pl.pallas_call(
        functools.partial(kernel, n_replica // GROUP, n_tensor, width, cache_len, key_rows),
        out_shape=(out, out),
        in_specs=[pl.BlockSpec(memory_space=pltpu.SMEM)]
        + [pl.BlockSpec(memory_space=pltpu.HBM)] * 13,
        out_specs=(pl.BlockSpec(memory_space=pltpu.HBM),) * 2,
        scratch_shapes=[
            pltpu.VMEM(new_down_q.shape, BF16),
            pltpu.VMEM(refreshed_query_up.shape, BF16),
            pltpu.VMEM(new_down_o.shape, BF16),
            pltpu.VMEM(new_up_o.shape, BF16),
            pltpu.VMEM((STEPS, ROWS, width), BF16),
            pltpu.VMEM((STEPS, ROWS, width), BF16),
            pltpu.VMEM(base_key_value.shape, BF16),
            pltpu.VMEM((ROWS, key_rows, HD), BF16),
            pltpu.VMEM((ROWS, key_rows, HD), BF16),
            pltpu.VMEM((4, RANK, width), BF16),
            pltpu.VMEM((4, RANK, width), BF16),
            pltpu.VMEM((2, 2 * tiles, LANES), BF16),
            pltpu.VMEM((2, GROUP, 2 * tiles, LANES), BF16),
            pltpu.VMEM((2, 2 * tiles, LANES), F32),
            pltpu.VMEM((GROUP * 2 * tiles, LANES), F32),
            pltpu.VMEM((2, ROWS * ROWS, HD), F32),
            pltpu.VMEM((STEPS, width // HD * ROWS, HD), F32),
            pltpu.VMEM((STEPS, width // HD * ROWS, HD), F32),
            pltpu.VMEM((2, 2 * ROWS, LANES), F32),
            pltpu.VMEM((2, n_tensor, 2 * ROWS, LANES), F32),
            pltpu.VMEM((STEPS, ROWS, width), BF16),
            pltpu.VMEM((STEPS, ROWS, width), BF16),
            pltpu.SMEM(lengths.shape, jnp.int32),
            dma((14,)),
            dma((2, ROWS)),
            dma((2,)),
            dma((2,)),
            dma((4,)),
            dma((4,)),
            dma((2,)),
            dma((2,)),
        ],
        compiler_params=pltpu.CompilerParams(
            collective_id=0, has_side_effects=True, vmem_limit_bytes=60 * 1024 * 1024
        ),
    )(
        switch_step, lengths, hidden_in, frozen_query_rows, base_key_value, cache,
        old_down_q, current_query_up, old_down_o, old_up_o,
        new_down_q, refreshed_query_up, new_down_o, new_up_o,
    )


def solution(mesh):
    placed = (
        P(None, "replica", None),
        P(None, "replica", "tensor"),
        P(None, None, "replica", "tensor"),
        P(None, "replica", None, "tensor"),
        P("replica"),
        P("replica"),
        P(),
        P(None, "tensor"),
        P(None, "tensor"),
        P(),
        P("replica", None),
        P("replica", "tensor"),
        P("replica", "tensor"),
        P("replica", None),
    )
    return jax.shard_map(
        functools.partial(body, mesh.shape["replica"], mesh.shape["tensor"]),
        mesh=mesh,
        in_specs=placed,
        out_specs=(P(None, "replica", "tensor"), P(None, "replica", "tensor")),
        check_vma=False,
    )
```

```python
import functools

import jax
import jax.numpy as jnp
from jax import lax
from jax.experimental import pallas as pl
from jax.experimental.pallas import tpu as pltpu
from jax.sharding import PartitionSpec as P

HD = 128
STEPS = 3
ROWS = 8
RANK = 64
GROUP = 16
LANES = 128
MESH = pl.DeviceIdType.MESH
F32 = jnp.float32
BF16 = jnp.bfloat16


def nt(a, b):
    return lax.dot_general(a, b, (((1,), (1,)), ((), ())), preferred_element_type=F32)


def nn(a, b):
    return lax.dot_general(a, b, (((1,), (0,)), ((), ())), preferred_element_type=F32)


def kernel(
    n_block, n_tensor, width, cache_len, key_rows,
    switch, lengths_in, hidden, frozen, fresh, cache,
    old_dq, old_uq, old_do, old_uo, new_dq, new_uq, new_do, new_uo,
    attended_out, adapter_out,
    row_dq, row_uq, row_do, row_uo, hid, frz, frs, kbuf, vbuf,
    w_old, w_new, packs, landed, stage, spread, fresh_rows, q_heads, a_rows,
    part, parts, lengths,
    loc, kv_sem, s1_send, s1_recv, s2_send, s2_recv, ar_send, ar_recv,
):
    replica = lax.axis_index("replica")
    tensor = lax.axis_index("tensor")
    mine = lax.rem(replica, GROUP)
    block = lax.div(replica, GROUP)
    base = block * GROUP
    cols = pl.ds(pl.multiple_of(tensor * width, width), width)
    heads = width // HD
    tiles = width // LANES

    group_peers = [
        (base + lax.rem(mine + GROUP // 2 + j, GROUP), tensor)
        for j in sorted(range(1 - GROUP // 2, GROUP // 2), key=abs)
    ]
    block_peers = [
        (lax.rem(block + j, n_block) * GROUP + mine, tensor) for j in (2, 1, 3)
    ]
    tensor_peers = [(replica, lax.rem(tensor + j, n_tensor)) for j in (4, 3, 5, 2, 6, 1, 7)]
    barrier = pltpu.get_barrier_semaphore()
    everyone = group_peers + block_peers + tensor_peers
    for peer in everyone:
        pl.semaphore_signal(barrier, inc=1, device_id=peer, device_id_type=MESH)

    local = [
        pltpu.make_async_copy(new_dq, row_dq, loc.at[0]),
        pltpu.make_async_copy(new_uq, row_uq, loc.at[1]),
        pltpu.make_async_copy(new_do, row_do, loc.at[2]),
        pltpu.make_async_copy(new_uo, row_uo, loc.at[3]),
        pltpu.make_async_copy(hidden.at[:, :, cols], hid, loc.at[4]),
        pltpu.make_async_copy(old_dq.at[:, cols], w_old.at[0], loc.at[5]),
        pltpu.make_async_copy(fresh, frs, loc.at[6]),
        pltpu.make_async_copy(old_uq, w_old.at[1], loc.at[7]),
        pltpu.make_async_copy(frozen, frz, loc.at[8]),
        pltpu.make_async_copy(old_do, w_old.at[2], loc.at[9]),
        pltpu.make_async_copy(old_uo.at[:, cols], w_old.at[3], loc.at[10]),
        pltpu.make_async_copy(lengths_in, lengths, loc.at[11]),
    ]
    for copy in local[:5]:
        copy.start()
    kv = []
    for b in range(ROWS):
        kv.append(pltpu.make_async_copy(cache.at[0, b], kbuf.at[b, pl.ds(0, cache_len)], kv_sem.at[0, b]))
        kv.append(pltpu.make_async_copy(cache.at[1, b], vbuf.at[b, pl.ds(0, cache_len)], kv_sem.at[1, b]))

    for copy in local[:4]:
        copy.wait()
    for i, row in enumerate((row_dq[:, cols], row_uq[...], row_do[...], row_uo[:, cols])):
        row = row.astype(F32)
        for s in range(tiles):
            stage[i // 2, pl.ds((i % 2) * tiles + s, 1), :] = row[:, s * LANES : (s + 1) * LANES]
    for p in range(2):
        packs[p] = stage[p].astype(BF16)
        landed[p, mine] = packs[p]

    pl.semaphore_wait(barrier, len(everyone))

    for p in range(2):
        for peer in group_peers:
            pltpu.make_async_remote_copy(
                src_ref=packs.at[p],
                dst_ref=landed.at[p, mine],
                send_sem=s1_send.at[p],
                recv_sem=s1_recv.at[p],
                device_id=peer,
                device_id_type=MESH,
            ).start()

    for copy in local[5:] + kv:
        copy.start()

    local[6].wait()
    pad = key_rows - cache_len - 16
    for i, buf in enumerate((kbuf, vbuf)):
        for u in range(ROWS):
            if u < STEPS:
                fresh_rows[i, pl.ds(u * ROWS, ROWS), :] = frs[i, u].astype(F32)
            else:
                fresh_rows[i, pl.ds(u * ROWS, ROWS), :] = jnp.zeros((ROWS, HD), F32)
        for b in range(ROWS):
            rows = fresh_rows[i, pl.ds(b, ROWS, stride=ROWS), :]
            rows = jnp.concatenate([rows, jnp.zeros((8, HD), F32)], axis=0)
            buf[b, pl.ds(cache_len, 16), :] = rows.astype(BF16)
            buf[b, pl.ds(cache_len + 16, pad), :] = jnp.zeros((pad, HD), BF16)

    local[4].wait()
    hid_rows = jnp.concatenate([hid[t].astype(F32) for t in range(STEPS)], axis=0).astype(BF16)

    own_rows = pl.ds(pl.multiple_of(block * GROUP, GROUP), GROUP)

    def gathered(p):
        pltpu.make_async_copy(
            landed.at[p, pl.ds(0, GROUP - 1)], landed.at[p, pl.ds(0, GROUP - 1)], s1_recv.at[p]
        ).wait()
        spread[...] = landed[p].reshape(GROUP * 2 * tiles, LANES).astype(F32)
        for half in range(2):
            m = 2 * p + half
            for s in range(tiles):
                w_new[m, own_rows, s * LANES : (s + 1) * LANES] = spread[
                    pl.ds(half * tiles + s, GROUP, stride=2 * tiles), :
                ].astype(BF16)
            for peer in block_peers:
                pltpu.make_async_remote_copy(
                    src_ref=w_new.at[m, own_rows],
                    dst_ref=w_new.at[m, own_rows],
                    send_sem=s2_send.at[m],
                    recv_sem=s2_recv.at[m],
                    device_id=peer,
                    device_id_type=MESH,
                ).start()

    def weights(m):
        others = w_new.at[m, pl.ds(0, (n_block - 1) * GROUP)]
        pltpu.make_async_copy(others, others, s2_recv.at[m]).wait()
        return jnp.concatenate([w_old[m], w_new[m]], axis=0)

    lane_half = lax.div(lax.broadcasted_iota(jnp.int32, (ROWS, LANES), 1), RANK)
    switch_at = jnp.full((ROWS, LANES), switch[0], jnp.int32)
    half_of = [jnp.where(switch_at <= t, 1, 0) for t in range(STEPS)]

    def reduce_start(r, product):
        chosen = []
        for t in range(STEPS):
            rows = product[t * ROWS : (t + 1) * ROWS]
            chosen.append(jnp.where(half_of[t] == t % 2, rows, pltpu.roll(rows, RANK, 1)))
        tile = jnp.concatenate([jnp.where(lane_half == 0, chosen[0], chosen[1]), chosen[2]], axis=0)
        part[r] = tile
        parts[r, tensor] = tile
        for peer in tensor_peers:
            pltpu.make_async_remote_copy(
                src_ref=part.at[r],
                dst_ref=parts.at[r, tensor],
                send_sem=ar_send.at[r],
                recv_sem=ar_recv.at[r],
                device_id=peer,
                device_id_type=MESH,
            ).start()

    def reduce_done(r):
        others = parts.at[r, pl.ds(0, n_tensor - 1)]
        pltpu.make_async_copy(others, others, ar_recv.at[r]).wait()
        total = jnp.sum(parts[r], axis=0)
        rows = []
        for t in range(STEPS):
            tile = total[(t // 2) * ROWS : (t // 2 + 1) * ROWS]
            both = jnp.where(lane_half == t % 2, tile, pltpu.roll(tile, RANK, 1))
            rows.append(jnp.where(lane_half == half_of[t], both, 0.0))
        return jnp.concatenate(rows, axis=0).astype(BF16)

    gathered(0)
    gathered(1)

    local[5].wait()
    reduce_start(0, nt(hid_rows, weights(0)))

    local[7].wait()
    local[8].wait()
    up_q = weights(1)
    for copy in kv:
        copy.wait()
    local[11].wait()
    low_rank = reduce_done(0)
    delta = nn(low_rank, up_q)
    for t in range(STEPS):
        for h in range(heads):
            at = slice(h * HD, (h + 1) * HD)
            q_heads[t, pl.ds(h * ROWS, ROWS), :] = (
                frz[t, :, at].astype(F32) + delta[t * ROWS : (t + 1) * ROWS, at]
            )

    scale = 1.0 / HD**0.5
    query_rows = STEPS * heads
    col = lax.broadcasted_iota(jnp.int32, (query_rows, key_rows), 1)
    row = lax.broadcasted_iota(jnp.int32, (query_rows, key_rows), 0)
    is_fresh = jnp.logical_and(col >= cache_len, (col - cache_len) * heads <= row)
    for b in range(ROWS):
        query = jnp.concatenate(
            [q_heads[t, pl.ds(b, heads, stride=ROWS), :] for t in range(STEPS)], axis=0
        ).astype(BF16)
        scores = nt(query, kbuf[b]) * scale
        live = jnp.logical_or(col < lengths[b], is_fresh)
        scores = jnp.where(live, scores, -1e30)
        top = jnp.max(scores, axis=1, keepdims=True)
        exps = jnp.exp(scores - top)
        total = jnp.sum(exps, axis=1, keepdims=True)
        probs = (exps * (1.0 / total)).astype(BF16)
        result = nn(probs, vbuf[b])
        for t in range(STEPS):
            a_rows[t, pl.ds(b * heads, heads), :] = result[t * heads : (t + 1) * heads]

    attended = []
    for t in range(STEPS):
        rows = jnp.concatenate(
            [a_rows[t, pl.ds(h, ROWS, stride=heads), :] for h in range(heads)], axis=1
        )
        attended.append(rows)
        attended_out[t] = rows.astype(BF16)

    local[9].wait()
    reduce_start(1, nt(jnp.concatenate(attended, axis=0).astype(BF16), weights(2)))
    local[10].wait()
    up_o = weights(3)
    result = nn(reduce_done(1), up_o)
    for t in range(STEPS):
        adapter_out[t] = result[t * ROWS : (t + 1) * ROWS].astype(BF16)

    for p in range(2):
        sent = landed.at[p, pl.ds(0, GROUP - 1)]
        pltpu.make_async_copy(sent, sent, s1_send.at[p]).wait()
    for m in range(4):
        sent = w_new.at[m, pl.ds(0, (n_block - 1) * GROUP)]
        pltpu.make_async_copy(sent, sent, s2_send.at[m]).wait()
    for r in range(2):
        sent = parts.at[r, pl.ds(0, n_tensor - 1)]
        pltpu.make_async_copy(sent, sent, ar_send.at[r]).wait()


def body(
    n_replica, n_tensor,
    hidden_in, frozen_query_rows, base_key_value, cache, lengths, switch_step,
    old_down_q, current_query_up, old_down_o, old_up_o,
    new_down_q, refreshed_query_up, new_down_o, new_up_o,
):
    width = frozen_query_rows.shape[-1]
    cache_len = cache.shape[2]
    key_rows = cache_len + LANES
    tiles = width // LANES
    dma = pltpu.SemaphoreType.DMA
    out = pltpu.VMEM(frozen_query_rows.shape, BF16)
    return pl.pallas_call(
        functools.partial(kernel, n_replica // GROUP, n_tensor, width, cache_len, key_rows),
        out_shape=(out, out),
        in_specs=[pl.BlockSpec(memory_space=pltpu.SMEM)]
        + [pl.BlockSpec(memory_space=pltpu.HBM)] * 13,
        out_specs=(pl.BlockSpec(memory_space=pltpu.VMEM),) * 2,
        scratch_shapes=[
            pltpu.VMEM(new_down_q.shape, BF16),
            pltpu.VMEM(refreshed_query_up.shape, BF16),
            pltpu.VMEM(new_down_o.shape, BF16),
            pltpu.VMEM(new_up_o.shape, BF16),
            pltpu.VMEM((STEPS, ROWS, width), BF16),
            pltpu.VMEM((STEPS, ROWS, width), BF16),
            pltpu.VMEM(base_key_value.shape, BF16),
            pltpu.VMEM((ROWS, key_rows, HD), BF16),
            pltpu.VMEM((ROWS, key_rows, HD), BF16),
            pltpu.VMEM((4, RANK, width), BF16),
            pltpu.VMEM((4, RANK, width), BF16),
            pltpu.VMEM((2, 2 * tiles, LANES), BF16),
            pltpu.VMEM((2, GROUP, 2 * tiles, LANES), BF16),
            pltpu.VMEM((2, 2 * tiles, LANES), F32),
            pltpu.VMEM((GROUP * 2 * tiles, LANES), F32),
            pltpu.VMEM((2, ROWS * ROWS, HD), F32),
            pltpu.VMEM((STEPS, width // HD * ROWS, HD), F32),
            pltpu.VMEM((STEPS, width // HD * ROWS, HD), F32),
            pltpu.VMEM((2, 2 * ROWS, LANES), F32),
            pltpu.VMEM((2, n_tensor, 2 * ROWS, LANES), F32),
            pltpu.SMEM(lengths.shape, jnp.int32),
            dma((12,)),
            dma((2, ROWS)),
            dma((2,)),
            dma((2,)),
            dma((4,)),
            dma((4,)),
            dma((2,)),
            dma((2,)),
        ],
        compiler_params=pltpu.CompilerParams(
            collective_id=0, has_side_effects=True, vmem_limit_bytes=32 * 1024 * 1024
        ),
    )(
        switch_step,
        *[
            pltpu.with_memory_space_constraint(operand, pltpu.HBM)
            for operand in (
                lengths, hidden_in, frozen_query_rows, base_key_value, cache,
                old_down_q, current_query_up, old_down_o, old_up_o,
                new_down_q, refreshed_query_up, new_down_o, new_up_o,
            )
        ],
    )


def solution(mesh):
    placed = (
        P(None, "replica", None),
        P(None, "replica", "tensor"),
        P(None, None, "replica", "tensor"),
        P(None, "replica", None, "tensor"),
        P("replica"),
        P("replica"),
        P(),
        P(None, "tensor"),
        P(None, "tensor"),
        P(),
        P("replica", None),
        P("replica", "tensor"),
        P("replica", "tensor"),
        P("replica", None),
    )
    return jax.shard_map(
        functools.partial(body, mesh.shape["replica"], mesh.shape["tensor"]),
        mesh=mesh,
        in_specs=placed,
        out_specs=(P(None, "replica", "tensor"), P(None, "replica", "tensor")),
        check_vma=False,
    )
```

```python
import functools

import jax
import jax.numpy as jnp
from jax import lax
from jax.experimental import pallas as pl
from jax.experimental.pallas import tpu as pltpu
from jax.sharding import PartitionSpec as P

HD = 128
STEPS = 3
ROWS = 8
RANK = 64
GROUP = 16
LANES = 128
MESH = pl.DeviceIdType.MESH
F32 = jnp.float32
BF16 = jnp.bfloat16


def nt(a, b):
    return lax.dot_general(a, b, (((1,), (1,)), ((), ())), preferred_element_type=F32)


def nn(a, b):
    return lax.dot_general(a, b, (((1,), (0,)), ((), ())), preferred_element_type=F32)


def kernel(
    n_block, n_tensor, width, cache_len, key_rows,
    switch, lengths_in, hidden, frozen, fresh, cache,
    old_dq, old_uq, old_do, old_uo, new_dq, new_uq, new_do, new_uo,
    attended_out, adapter_out,
    row_dq, row_uq, row_do, row_uo, hid_own, hid_rows, hid_full, dq_full, frz, frs, kbuf, vbuf,
    w_old, w_new, packs, landed, stage, spread, fresh_rows, old_rank, q_heads, a_rows,
    rank_part, rank_parts, part, parts, lengths,
    loc, kv_sem, s1_send, s1_recv, hid_send, hid_recv, s2_send, s2_recv,
    rank_send, rank_recv, sum_send, sum_recv,
):
    replica = lax.axis_index("replica")
    tensor = lax.axis_index("tensor")
    mine = lax.rem(replica, GROUP)
    block = lax.div(replica, GROUP)
    base = block * GROUP
    cols = pl.ds(pl.multiple_of(tensor * width, width), width)
    heads = width // HD
    tiles = width // LANES

    def block_at(j):
        return lax.rem(block + j, n_block)

    def tensor_at(j):
        return lax.rem(tensor + j, n_tensor)

    block_order = sorted(range(n_block), key=lambda j: -min(j, n_block - j))
    tensor_order = sorted(range(n_tensor), key=lambda j: -min(j, n_tensor - j))
    group_peers = [
        (base + lax.rem(mine + GROUP // 2 + j, GROUP), tensor)
        for j in sorted(range(1 - GROUP // 2, GROUP // 2), key=abs)
    ]
    block_peers = [(block_at(j) * GROUP + mine, tensor) for j in block_order if j]
    tensor_peers = [(replica, tensor_at(j)) for j in tensor_order if j]
    rank_peers = [
        (block_at(i), (block_at(i) * GROUP + mine, tensor_at(j)))
        for i in block_order
        for j in tensor_order
        if i or j
    ]
    barrier = pltpu.get_barrier_semaphore()
    everyone = group_peers + [peer for _, peer in rank_peers]
    for peer in everyone:
        pl.semaphore_signal(barrier, inc=1, device_id=peer, device_id_type=MESH)

    def send(src, dst, send_sem, recv_sem, peer):
        pltpu.make_async_remote_copy(
            src_ref=src,
            dst_ref=dst,
            send_sem=send_sem,
            recv_sem=recv_sem,
            device_id=peer,
            device_id_type=MESH,
        ).start()

    def wait_bytes(ref, sem):
        pltpu.make_async_copy(ref, ref, sem).wait()

    local = [
        pltpu.make_async_copy(new_dq, row_dq, loc.at[0]),
        pltpu.make_async_copy(new_uq, row_uq, loc.at[1]),
        pltpu.make_async_copy(new_do, row_do, loc.at[2]),
        pltpu.make_async_copy(new_uo, row_uo, loc.at[3]),
        pltpu.make_async_copy(hidden.at[:, :, cols], hid_own.at[block], loc.at[4]),
        pltpu.make_async_copy(fresh, frs, loc.at[5]),
        pltpu.make_async_copy(hidden, hid_full, loc.at[6]),
        pltpu.make_async_copy(old_dq, dq_full, loc.at[7]),
        pltpu.make_async_copy(old_uq, w_old.at[0], loc.at[8]),
        pltpu.make_async_copy(frozen, frz, loc.at[9]),
        pltpu.make_async_copy(old_do, w_old.at[1], loc.at[10]),
        pltpu.make_async_copy(old_uo.at[:, cols], w_old.at[2], loc.at[11]),
        pltpu.make_async_copy(lengths_in, lengths, loc.at[12]),
    ]
    for copy in local[:5]:
        copy.start()
    kv = []
    for b in range(ROWS):
        kv.append(pltpu.make_async_copy(cache.at[0, b], kbuf.at[b, pl.ds(0, cache_len)], kv_sem.at[0, b]))
        kv.append(pltpu.make_async_copy(cache.at[1, b], vbuf.at[b, pl.ds(0, cache_len)], kv_sem.at[1, b]))

    for copy in local[:4]:
        copy.wait()
    for i, row in enumerate((row_dq[:, cols], row_uq[...], row_do[...], row_uo[:, cols])):
        row = row.astype(F32)
        for s in range(tiles):
            stage[i // 2, pl.ds((i % 2) * tiles + s, 1), :] = row[:, s * LANES : (s + 1) * LANES]
    for p in range(2):
        packs[p] = stage[p].astype(BF16)
        landed[p, mine] = packs[p]

    pl.semaphore_wait(barrier, len(everyone))

    for peer in group_peers:
        send(packs.at[0], landed.at[0, mine], s1_send.at[0], s1_recv.at[0], peer)
    local[4].wait()
    for peer in block_peers:
        send(hid_own.at[block], hid_own.at[block], hid_send, hid_recv, peer)
    for peer in group_peers:
        send(packs.at[1], landed.at[1, mine], s1_send.at[1], s1_recv.at[1], peer)

    for copy in local[5:] + kv:
        copy.start()

    local[5].wait()
    pad = key_rows - cache_len - 16
    for i, buf in enumerate((kbuf, vbuf)):
        for u in range(ROWS):
            if u < STEPS:
                fresh_rows[i, pl.ds(u * ROWS, ROWS), :] = frs[i, u].astype(F32)
            else:
                fresh_rows[i, pl.ds(u * ROWS, ROWS), :] = jnp.zeros((ROWS, HD), F32)
        for b in range(ROWS):
            rows = fresh_rows[i, pl.ds(b, ROWS, stride=ROWS), :]
            rows = jnp.concatenate([rows, jnp.zeros((8, HD), F32)], axis=0)
            buf[b, pl.ds(cache_len, 16), :] = rows.astype(BF16)
            buf[b, pl.ds(cache_len + 16, pad), :] = jnp.zeros((pad, HD), BF16)

    wait_bytes(hid_own.at[pl.ds(0, n_block - 1)], hid_recv)
    for k in range(n_block):
        rows = jnp.concatenate([hid_own[k, t].astype(F32) for t in range(STEPS)], axis=0)
        hid_rows[pl.ds(k * STEPS * ROWS, STEPS * ROWS), :] = rows.astype(BF16)

    own_rows = pl.ds(pl.multiple_of(block * GROUP, GROUP), GROUP)
    lane = lax.broadcasted_iota(jnp.int32, (ROWS, LANES), 1)
    lane_half = lax.div(lane, RANK)
    lane_group = lax.div(lane, GROUP)

    def arrived(p):
        wait_bytes(landed.at[p, pl.ds(0, GROUP - 1)], s1_recv.at[p])
        spread[p] = landed[p].reshape(GROUP * 2 * tiles, LANES).astype(F32)

    def rows_of(i):
        return [
            spread[i // 2, pl.ds((i % 2) * tiles + s, GROUP, stride=2 * tiles), :].astype(BF16)
            for s in range(tiles)
        ]

    def share(m):
        for s, tile in enumerate(rows_of(m + 1)):
            w_new[m, own_rows, s * LANES : (s + 1) * LANES] = tile
        for peer in block_peers:
            send(w_new.at[m, own_rows], w_new.at[m, own_rows], s2_send.at[m], s2_recv.at[m], peer)

    def weights(m):
        wait_bytes(w_new.at[m, pl.ds(0, (n_block - 1) * GROUP)], s2_recv.at[m])
        return jnp.concatenate([w_old[m], w_new[m]], axis=0)

    arrived(0)
    down_q = jnp.concatenate(rows_of(0), axis=1)
    ranks = nt(hid_rows[...], jnp.concatenate([down_q] * (LANES // GROUP), axis=0))
    for k in range(n_block):
        tile = jnp.zeros((ROWS, LANES), F32)
        for t in range(STEPS):
            at = (k * STEPS + t) * ROWS
            tile = jnp.where(lane_group == t, ranks[at : at + ROWS], tile)
        rank_part[k] = tile
    slot = block * n_tensor + tensor
    rank_parts[slot] = rank_part[block]
    for k, peer in rank_peers:
        send(rank_part.at[k], rank_parts.at[slot], rank_send, rank_recv, peer)

    share(0)
    arrived(1)
    share(1)
    share(2)

    local[6].wait()
    local[7].wait()
    old_rank[...] = jnp.zeros_like(old_rank)
    old = jnp.zeros((STEPS * ROWS, RANK), F32)
    for c in range(n_tensor):
        at = slice(c * width, (c + 1) * width)
        rows = jnp.concatenate([hid_full[t, :, at].astype(F32) for t in range(STEPS)], axis=0)
        old = old + nt(rows.astype(BF16), dq_full[:, at])
    old_rank[:, 0:RANK] = old

    switch_at = jnp.full((ROWS, LANES), switch[0], jnp.int32)
    half_of = [jnp.where(switch_at <= t, 1, 0) for t in range(STEPS)]

    for i in (8, 9, 10, 11, 12):
        local[i].wait()
    for copy in kv:
        copy.wait()

    wait_bytes(rank_parts.at[pl.ds(0, n_block * n_tensor - 1)], rank_recv)
    sums = [
        jnp.sum(rank_parts[k * n_tensor : (k + 1) * n_tensor], axis=0) for k in range(n_block)
    ]
    chosen = []
    for t in range(STEPS):
        both = old_rank[t * ROWS : (t + 1) * ROWS]
        for k in range(n_block):
            at = RANK // GROUP + k
            moved = pltpu.roll(sums[k], (at - t) * GROUP, 1)
            both = jnp.where(lane_group == at, moved, both)
        chosen.append(jnp.where(lane_half == half_of[t], both, 0.0))
    low_rank = jnp.concatenate(chosen, axis=0).astype(BF16)
    delta = nn(low_rank, weights(0))
    for t in range(STEPS):
        for h in range(heads):
            at = slice(h * HD, (h + 1) * HD)
            q_heads[t, pl.ds(h * ROWS, ROWS), :] = (
                frz[t, :, at].astype(F32) + delta[t * ROWS : (t + 1) * ROWS, at]
            )

    scale = 1.0 / HD**0.5
    query_rows = STEPS * heads
    col = lax.broadcasted_iota(jnp.int32, (query_rows, key_rows), 1)
    row = lax.broadcasted_iota(jnp.int32, (query_rows, key_rows), 0)
    is_fresh = jnp.logical_and(col >= cache_len, (col - cache_len) * heads <= row)
    for b in range(ROWS):
        query = jnp.concatenate(
            [q_heads[t, pl.ds(b, heads, stride=ROWS), :] for t in range(STEPS)], axis=0
        ).astype(BF16)
        scores = nt(query, kbuf[b]) * scale
        live = jnp.logical_or(col < lengths[b], is_fresh)
        scores = jnp.where(live, scores, -1e30)
        top = jnp.max(scores, axis=1, keepdims=True)
        exps = jnp.exp(scores - top)
        total = jnp.sum(exps, axis=1, keepdims=True)
        probs = (exps * (1.0 / total)).astype(BF16)
        result = nn(probs, vbuf[b])
        for t in range(STEPS):
            a_rows[t, pl.ds(b * heads, heads), :] = result[t * heads : (t + 1) * heads]

    attended = []
    for t in range(STEPS):
        rows = jnp.concatenate(
            [a_rows[t, pl.ds(h, ROWS, stride=heads), :] for h in range(heads)], axis=1
        )
        attended.append(rows)
        attended_out[t] = rows.astype(BF16)

    product = nt(jnp.concatenate(attended, axis=0).astype(BF16), weights(1))
    picked = []
    for t in range(STEPS):
        rows = product[t * ROWS : (t + 1) * ROWS]
        picked.append(jnp.where(half_of[t] == t % 2, rows, pltpu.roll(rows, RANK, 1)))
    tile = jnp.concatenate([jnp.where(lane_half == 0, picked[0], picked[1]), picked[2]], axis=0)
    part[...] = tile
    parts[tensor] = tile
    for peer in tensor_peers:
        send(part, parts.at[tensor], sum_send, sum_recv, peer)

    up_o = weights(2)
    wait_bytes(parts.at[pl.ds(0, n_tensor - 1)], sum_recv)
    total = jnp.sum(parts[...], axis=0)
    rows = []
    for t in range(STEPS):
        tile = total[(t // 2) * ROWS : (t // 2 + 1) * ROWS]
        both = jnp.where(lane_half == t % 2, tile, pltpu.roll(tile, RANK, 1))
        rows.append(jnp.where(lane_half == half_of[t], both, 0.0))
    result = nn(jnp.concatenate(rows, axis=0).astype(BF16), up_o)
    for t in range(STEPS):
        adapter_out[t] = result[t * ROWS : (t + 1) * ROWS].astype(BF16)

    for p in range(2):
        wait_bytes(landed.at[p, pl.ds(0, GROUP - 1)], s1_send.at[p])
    wait_bytes(hid_own.at[pl.ds(0, n_block - 1)], hid_send)
    for m in range(3):
        wait_bytes(w_new.at[m, pl.ds(0, (n_block - 1) * GROUP)], s2_send.at[m])
    wait_bytes(rank_parts.at[pl.ds(0, n_block * n_tensor - 1)], rank_send)
    wait_bytes(parts.at[pl.ds(0, n_tensor - 1)], sum_send)


def body(
    n_replica, n_tensor,
    hidden_in, frozen_query_rows, base_key_value, cache, lengths, switch_step,
    old_down_q, current_query_up, old_down_o, old_up_o,
    new_down_q, refreshed_query_up, new_down_o, new_up_o,
):
    width = frozen_query_rows.shape[-1]
    cache_len = cache.shape[2]
    key_rows = cache_len + LANES
    tiles = width // LANES
    n_block = n_replica // GROUP
    dma = pltpu.SemaphoreType.DMA
    out = pltpu.VMEM(frozen_query_rows.shape, BF16)
    return pl.pallas_call(
        functools.partial(kernel, n_block, n_tensor, width, cache_len, key_rows),
        out_shape=(out, out),
        in_specs=[pl.BlockSpec(memory_space=pltpu.SMEM)]
        + [pl.BlockSpec(memory_space=pltpu.HBM)] * 13,
        out_specs=(pl.BlockSpec(memory_space=pltpu.VMEM),) * 2,
        scratch_shapes=[
            pltpu.VMEM(new_down_q.shape, BF16),
            pltpu.VMEM(refreshed_query_up.shape, BF16),
            pltpu.VMEM(new_down_o.shape, BF16),
            pltpu.VMEM(new_up_o.shape, BF16),
            pltpu.VMEM((n_block, STEPS, ROWS, width), BF16),
            pltpu.VMEM((n_block * STEPS * ROWS, width), BF16),
            pltpu.VMEM(hidden_in.shape, BF16),
            pltpu.VMEM(old_down_q.shape, BF16),
            pltpu.VMEM((STEPS, ROWS, width), BF16),
            pltpu.VMEM(base_key_value.shape, BF16),
            pltpu.VMEM((ROWS, key_rows, HD), BF16),
            pltpu.VMEM((ROWS, key_rows, HD), BF16),
            pltpu.VMEM((3, RANK, width), BF16),
            pltpu.VMEM((3, RANK, width), BF16),
            pltpu.VMEM((2, 2 * tiles, LANES), BF16),
            pltpu.VMEM((2, GROUP, 2 * tiles, LANES), BF16),
            pltpu.VMEM((2, 2 * tiles, LANES), F32),
            pltpu.VMEM((2, GROUP * 2 * tiles, LANES), F32),
            pltpu.VMEM((2, ROWS * ROWS, HD), F32),
            pltpu.VMEM((STEPS * ROWS, LANES), F32),
            pltpu.VMEM((STEPS, width // HD * ROWS, HD), F32),
            pltpu.VMEM((STEPS, width // HD * ROWS, HD), F32),
            pltpu.VMEM((n_block, ROWS, LANES), F32),
            pltpu.VMEM((n_block * n_tensor, ROWS, LANES), F32),
            pltpu.VMEM((2 * ROWS, LANES), F32),
            pltpu.VMEM((n_tensor, 2 * ROWS, LANES), F32),
            pltpu.SMEM(lengths.shape, jnp.int32),
            dma((13,)),
            dma((2, ROWS)),
            dma((2,)),
            dma((2,)),
            dma(()),
            dma(()),
            dma((3,)),
            dma((3,)),
            dma(()),
            dma(()),
            dma(()),
            dma(()),
        ],
        compiler_params=pltpu.CompilerParams(
            collective_id=0, has_side_effects=True, vmem_limit_bytes=32 * 1024 * 1024
        ),
    )(
        switch_step,
        *[
            pltpu.with_memory_space_constraint(operand, pltpu.HBM)
            for operand in (
                lengths, hidden_in, frozen_query_rows, base_key_value, cache,
                old_down_q, current_query_up, old_down_o, old_up_o,
                new_down_q, refreshed_query_up, new_down_o, new_up_o,
            )
        ],
    )


def solution(mesh):
    placed = (
        P(None, "replica", None),
        P(None, "replica", "tensor"),
        P(None, None, "replica", "tensor"),
        P(None, "replica", None, "tensor"),
        P("replica"),
        P("replica"),
        P(),
        P(None, "tensor"),
        P(None, "tensor"),
        P(),
        P("replica", None),
        P("replica", "tensor"),
        P("replica", "tensor"),
        P("replica", None),
    )
    return jax.shard_map(
        functools.partial(body, mesh.shape["replica"], mesh.shape["tensor"]),
        mesh=mesh,
        in_specs=placed,
        out_specs=(P(None, "replica", "tensor"), P(None, "replica", "tensor")),
        check_vma=False,
    )
```

```python
import functools

import jax
import jax.numpy as jnp
from jax import lax
from jax.experimental import pallas as pl
from jax.experimental.pallas import tpu as pltpu
from jax.sharding import PartitionSpec as P

HD = 128
STEPS = 3
ROWS = 8
RANK = 64
GROUP = 16
LANES = 128
MESH = pl.DeviceIdType.MESH
F32 = jnp.float32
BF16 = jnp.bfloat16


def nt(a, b):
    return lax.dot_general(a, b, (((1,), (1,)), ((), ())), preferred_element_type=F32)


def nn(a, b):
    return lax.dot_general(a, b, (((1,), (0,)), ((), ())), preferred_element_type=F32)


def kernel(
    n_block, n_tensor, width, cache_len, key_rows,
    switch, lengths_in, hidden, frozen, fresh, cache,
    old_dq, old_uq, old_do, old_uo, new_dq, new_uq, new_do, new_uo,
    attended_out, adapter_out,
    row_dq, row_uq, row_do, row_uo, hid_own, hid_rows, hid_full, dq_full, frz, frs, kbuf, vbuf,
    w_old, w_new, packs, landed, stage, spread, fresh_rows, old_rank, q_heads, a_rows,
    rank_part, rank_parts, part, parts, lengths,
    loc, kv_sem, s1_send, s1_recv, hid_send, hid_recv, s2_send, s2_recv,
    rank_send, rank_recv, sum_send, sum_recv,
):
    replica = lax.axis_index("replica")
    tensor = lax.axis_index("tensor")
    mine = lax.rem(replica, GROUP)
    block = lax.div(replica, GROUP)
    base = block * GROUP
    cols = pl.ds(pl.multiple_of(tensor * width, width), width)
    heads = width // HD
    tiles = width // LANES

    def block_at(j):
        return lax.rem(block + j, n_block)

    def tensor_at(j):
        return lax.rem(tensor + j, n_tensor)

    block_order = sorted(range(n_block), key=lambda j: -min(j, n_block - j))
    tensor_order = sorted(range(n_tensor), key=lambda j: -min(j, n_tensor - j))
    group_peers = [
        (base + lax.rem(mine + GROUP // 2 + j, GROUP), tensor)
        for j in sorted(range(1 - GROUP // 2, GROUP // 2), key=abs)
    ]
    block_peers = [(block_at(j) * GROUP + mine, tensor) for j in block_order if j]
    tensor_peers = [(replica, tensor_at(j)) for j in tensor_order if j]
    rank_peers = [
        (block_at(i), (block_at(i) * GROUP + mine, tensor_at(j)))
        for i in block_order
        for j in tensor_order
        if i or j
    ]
    def send(src, dst, send_sem, recv_sem, peer):
        pltpu.make_async_remote_copy(
            src_ref=src,
            dst_ref=dst,
            send_sem=send_sem,
            recv_sem=recv_sem,
            device_id=peer,
            device_id_type=MESH,
        ).start()

    def wait_bytes(ref, sem):
        pltpu.make_async_copy(ref, ref, sem).wait()

    local = [
        pltpu.make_async_copy(new_dq, row_dq, loc.at[0]),
        pltpu.make_async_copy(new_uq, row_uq, loc.at[1]),
        pltpu.make_async_copy(new_do, row_do, loc.at[2]),
        pltpu.make_async_copy(new_uo, row_uo, loc.at[3]),
        pltpu.make_async_copy(hidden.at[:, :, cols], hid_own.at[block], loc.at[4]),
        pltpu.make_async_copy(fresh, frs, loc.at[5]),
        pltpu.make_async_copy(hidden, hid_full, loc.at[6]),
        pltpu.make_async_copy(old_dq, dq_full, loc.at[7]),
        pltpu.make_async_copy(old_uq, w_old.at[0], loc.at[8]),
        pltpu.make_async_copy(frozen, frz, loc.at[9]),
        pltpu.make_async_copy(old_do, w_old.at[1], loc.at[10]),
        pltpu.make_async_copy(old_uo.at[:, cols], w_old.at[2], loc.at[11]),
        pltpu.make_async_copy(lengths_in, lengths, loc.at[12]),
    ]
    for copy in local[:5]:
        copy.start()
    barrier = pltpu.get_barrier_semaphore()
    everyone = group_peers + block_peers + tensor_peers
    for peer in everyone:
        pl.semaphore_signal(barrier, inc=1, device_id=peer, device_id_type=MESH)
    kv = []
    for b in range(ROWS):
        kv.append(pltpu.make_async_copy(cache.at[0, b], kbuf.at[b, pl.ds(0, cache_len)], kv_sem.at[0, b]))
        kv.append(pltpu.make_async_copy(cache.at[1, b], vbuf.at[b, pl.ds(0, cache_len)], kv_sem.at[1, b]))

    def pack(p, rows):
        for i, row in enumerate(rows):
            row = row.astype(F32)
            for c in range(tiles):
                stage[p, pl.ds(i * tiles + c, 1), :] = row[:, c * LANES : (c + 1) * LANES]
        packs[p] = stage[p].astype(BF16)
        landed[p, mine] = packs[p]

    for copy in local[:2]:
        copy.wait()
    pack(0, (row_dq[:, cols], row_uq[...]))
    pl.semaphore_wait(barrier, len(everyone))
    for peer in group_peers:
        send(packs.at[0], landed.at[0, mine], s1_send.at[0], s1_recv.at[0], peer)
    local[4].wait()
    for peer in block_peers:
        send(hid_own.at[block], hid_own.at[block], hid_send, hid_recv, peer)
    for copy in local[2:4]:
        copy.wait()
    pack(1, (row_do[...], row_uo[:, cols]))
    for peer in group_peers:
        send(packs.at[1], landed.at[1, mine], s1_send.at[1], s1_recv.at[1], peer)

    for copy in local[5:] + kv:
        copy.start()

    local[5].wait()
    pad = key_rows - cache_len - 16
    for i, buf in enumerate((kbuf, vbuf)):
        for u in range(ROWS):
            if u < STEPS:
                fresh_rows[i, pl.ds(u * ROWS, ROWS), :] = frs[i, u].astype(F32)
            else:
                fresh_rows[i, pl.ds(u * ROWS, ROWS), :] = jnp.zeros((ROWS, HD), F32)
        for b in range(ROWS):
            rows = fresh_rows[i, pl.ds(b, ROWS, stride=ROWS), :]
            rows = jnp.concatenate([rows, jnp.zeros((8, HD), F32)], axis=0)
            buf[b, pl.ds(cache_len, 16), :] = rows.astype(BF16)
            buf[b, pl.ds(cache_len + 16, pad), :] = jnp.zeros((pad, HD), BF16)

    wait_bytes(hid_own.at[pl.ds(0, n_block - 1)], hid_recv)
    for k in range(n_block):
        rows = jnp.concatenate([hid_own[k, t].astype(F32) for t in range(STEPS)], axis=0)
        hid_rows[pl.ds(k * STEPS * ROWS, STEPS * ROWS), :] = rows.astype(BF16)

    own_rows = pl.ds(pl.multiple_of(block * GROUP, GROUP), GROUP)
    lane = lax.broadcasted_iota(jnp.int32, (ROWS, LANES), 1)
    lane_half = lax.div(lane, RANK)
    lane_group = lax.div(lane, GROUP)

    def arrived(p):
        wait_bytes(landed.at[p, pl.ds(0, GROUP - 1)], s1_recv.at[p])
        spread[p] = landed[p].reshape(GROUP * 2 * tiles, LANES).astype(F32)

    def rows_of(i):
        return [
            spread[i // 2, pl.ds((i % 2) * tiles + s, GROUP, stride=2 * tiles), :].astype(BF16)
            for s in range(tiles)
        ]

    def share(m):
        for s, tile in enumerate(rows_of(m + 1)):
            w_new[m, own_rows, s * LANES : (s + 1) * LANES] = tile
        for peer in block_peers:
            send(w_new.at[m, own_rows], w_new.at[m, own_rows], s2_send.at[m], s2_recv.at[m], peer)

    def weights(m):
        wait_bytes(w_new.at[m, pl.ds(0, (n_block - 1) * GROUP)], s2_recv.at[m])
        return jnp.concatenate([w_old[m], w_new[m]], axis=0)

    local[6].wait()
    local[7].wait()
    old_rank[...] = jnp.zeros_like(old_rank)
    old = jnp.zeros((STEPS * ROWS, RANK), F32)
    for c in range(n_tensor):
        at = slice(c * width, (c + 1) * width)
        rows = jnp.concatenate([hid_full[t, :, at].astype(F32) for t in range(STEPS)], axis=0)
        old = old + nt(rows.astype(BF16), dq_full[:, at])
    old_rank[:, 0:RANK] = old

    arrived(0)
    down_q = jnp.concatenate(rows_of(0), axis=1)
    ranks = nt(hid_rows[...], jnp.concatenate([down_q] * (LANES // GROUP), axis=0))
    for k in range(n_block):
        tile = jnp.zeros((ROWS, LANES), F32)
        for t in range(STEPS):
            at = (k * STEPS + t) * ROWS
            tile = jnp.where(lane_group == t, ranks[at : at + ROWS], tile)
        rank_part[k] = tile
    slot = block * n_tensor + tensor
    rank_parts[slot] = rank_part[block]
    for k, peer in rank_peers:
        send(rank_part.at[k], rank_parts.at[slot], rank_send, rank_recv, peer)

    share(0)
    arrived(1)
    share(1)
    share(2)

    switch_at = jnp.full((ROWS, LANES), switch[0], jnp.int32)
    half_of = [jnp.where(switch_at <= t, 1, 0) for t in range(STEPS)]

    for i in (8, 9, 10, 11, 12):
        local[i].wait()
    for copy in kv:
        copy.wait()

    wait_bytes(rank_parts.at[pl.ds(0, n_block * n_tensor - 1)], rank_recv)
    sums = [
        jnp.sum(rank_parts[k * n_tensor : (k + 1) * n_tensor], axis=0) for k in range(n_block)
    ]
    chosen = []
    for t in range(STEPS):
        both = old_rank[t * ROWS : (t + 1) * ROWS]
        for k in range(n_block):
            at = RANK // GROUP + k
            moved = pltpu.roll(sums[k], (at - t) * GROUP, 1)
            both = jnp.where(lane_group == at, moved, both)
        chosen.append(jnp.where(lane_half == half_of[t], both, 0.0))
    low_rank = jnp.concatenate(chosen, axis=0).astype(BF16)
    delta = nn(low_rank, weights(0))
    for t in range(STEPS):
        for h in range(heads):
            at = slice(h * HD, (h + 1) * HD)
            q_heads[t, pl.ds(h * ROWS, ROWS), :] = (
                frz[t, :, at].astype(F32) + delta[t * ROWS : (t + 1) * ROWS, at]
            )

    scale = 1.0 / HD**0.5
    query_rows = STEPS * heads
    col = lax.broadcasted_iota(jnp.int32, (query_rows, key_rows), 1)
    row = lax.broadcasted_iota(jnp.int32, (query_rows, key_rows), 0)
    is_fresh = jnp.logical_and(col >= cache_len, (col - cache_len) * heads <= row)
    queries = [
        jnp.concatenate([q_heads[t, pl.ds(b, heads, stride=ROWS), :] for t in range(STEPS)], axis=0).astype(BF16)
        for b in range(ROWS)
    ]
    scores = [nt(queries[b], kbuf[b]) for b in range(ROWS)]
    probs = []
    for b in range(ROWS):
        live = jnp.logical_or(col < lengths[b], is_fresh)
        shown = jnp.where(live, scores[b] * scale, -1e30)
        top = jnp.max(shown, axis=1, keepdims=True)
        exps = jnp.exp(shown - top)
        total = jnp.sum(exps, axis=1, keepdims=True)
        probs.append((exps * (1.0 / total)).astype(BF16))
    for b in range(ROWS):
        result = nn(probs[b], vbuf[b])
        for t in range(STEPS):
            a_rows[t, pl.ds(b * heads, heads), :] = result[t * heads : (t + 1) * heads]

    attended = []
    for t in range(STEPS):
        rows = jnp.concatenate(
            [a_rows[t, pl.ds(h, ROWS, stride=heads), :] for h in range(heads)], axis=1
        )
        attended.append(rows)
        attended_out[t] = rows.astype(BF16)

    product = nt(jnp.concatenate(attended, axis=0).astype(BF16), weights(1))
    picked = []
    for t in range(STEPS):
        rows = product[t * ROWS : (t + 1) * ROWS]
        picked.append(jnp.where(half_of[t] == t % 2, rows, pltpu.roll(rows, RANK, 1)))
    tile = jnp.concatenate([jnp.where(lane_half == 0, picked[0], picked[1]), picked[2]], axis=0)
    part[...] = tile
    parts[tensor] = tile
    for peer in tensor_peers:
        send(part, parts.at[tensor], sum_send, sum_recv, peer)

    up_o = weights(2)
    wait_bytes(parts.at[pl.ds(0, n_tensor - 1)], sum_recv)
    total = jnp.sum(parts[...], axis=0)
    rows = []
    for t in range(STEPS):
        tile = total[(t // 2) * ROWS : (t // 2 + 1) * ROWS]
        both = jnp.where(lane_half == t % 2, tile, pltpu.roll(tile, RANK, 1))
        rows.append(jnp.where(lane_half == half_of[t], both, 0.0))
    result = nn(jnp.concatenate(rows, axis=0).astype(BF16), up_o)
    for t in range(STEPS):
        adapter_out[t] = result[t * ROWS : (t + 1) * ROWS].astype(BF16)

    for p in range(2):
        wait_bytes(landed.at[p, pl.ds(0, GROUP - 1)], s1_send.at[p])
    wait_bytes(hid_own.at[pl.ds(0, n_block - 1)], hid_send)
    for m in range(3):
        wait_bytes(w_new.at[m, pl.ds(0, (n_block - 1) * GROUP)], s2_send.at[m])
    wait_bytes(rank_parts.at[pl.ds(0, n_block * n_tensor - 1)], rank_send)
    wait_bytes(parts.at[pl.ds(0, n_tensor - 1)], sum_send)


def write_out(attended, adapter, attended_out, adapter_out, sems):
    copies = [
        pltpu.make_async_copy(attended, attended_out, sems.at[0]),
        pltpu.make_async_copy(adapter, adapter_out, sems.at[1]),
    ]
    for copy in copies:
        copy.start()
    for copy in copies:
        copy.wait()


def body(
    n_replica, n_tensor,
    hidden_in, frozen_query_rows, base_key_value, cache, lengths, switch_step,
    old_down_q, current_query_up, old_down_o, old_up_o,
    new_down_q, refreshed_query_up, new_down_o, new_up_o,
):
    width = frozen_query_rows.shape[-1]
    cache_len = cache.shape[2]
    key_rows = cache_len + LANES
    tiles = width // LANES
    n_block = n_replica // GROUP
    dma = pltpu.SemaphoreType.DMA
    out = pltpu.VMEM(frozen_query_rows.shape, BF16)
    results = pl.pallas_call(
        functools.partial(kernel, n_block, n_tensor, width, cache_len, key_rows),
        out_shape=(out, out),
        in_specs=[pl.BlockSpec(memory_space=pltpu.SMEM)]
        + [pl.BlockSpec(memory_space=pltpu.HBM)] * 13,
        out_specs=(pl.BlockSpec(memory_space=pltpu.VMEM),) * 2,
        scratch_shapes=[
            pltpu.VMEM(new_down_q.shape, BF16),
            pltpu.VMEM(refreshed_query_up.shape, BF16),
            pltpu.VMEM(new_down_o.shape, BF16),
            pltpu.VMEM(new_up_o.shape, BF16),
            pltpu.VMEM((n_block, STEPS, ROWS, width), BF16),
            pltpu.VMEM((n_block * STEPS * ROWS, width), BF16),
            pltpu.VMEM(hidden_in.shape, BF16),
            pltpu.VMEM(old_down_q.shape, BF16),
            pltpu.VMEM((STEPS, ROWS, width), BF16),
            pltpu.VMEM(base_key_value.shape, BF16),
            pltpu.VMEM((ROWS, key_rows, HD), BF16),
            pltpu.VMEM((ROWS, key_rows, HD), BF16),
            pltpu.VMEM((3, RANK, width), BF16),
            pltpu.VMEM((3, RANK, width), BF16),
            pltpu.VMEM((2, 2 * tiles, LANES), BF16),
            pltpu.VMEM((2, GROUP, 2 * tiles, LANES), BF16),
            pltpu.VMEM((2, 2 * tiles, LANES), F32),
            pltpu.VMEM((2, GROUP * 2 * tiles, LANES), F32),
            pltpu.VMEM((2, ROWS * ROWS, HD), F32),
            pltpu.VMEM((STEPS * ROWS, LANES), F32),
            pltpu.VMEM((STEPS, width // HD * ROWS, HD), F32),
            pltpu.VMEM((STEPS, width // HD * ROWS, HD), F32),
            pltpu.VMEM((n_block, ROWS, LANES), F32),
            pltpu.VMEM((n_block * n_tensor, ROWS, LANES), F32),
            pltpu.VMEM((2 * ROWS, LANES), F32),
            pltpu.VMEM((n_tensor, 2 * ROWS, LANES), F32),
            pltpu.SMEM(lengths.shape, jnp.int32),
            dma((13,)),
            dma((2, ROWS)),
            dma((2,)),
            dma((2,)),
            dma(()),
            dma(()),
            dma((3,)),
            dma((3,)),
            dma(()),
            dma(()),
            dma(()),
            dma(()),
        ],
        compiler_params=pltpu.CompilerParams(
            collective_id=0, has_side_effects=True, vmem_limit_bytes=32 * 1024 * 1024
        ),
    )(
        switch_step,
        *[
            pltpu.with_memory_space_constraint(operand, pltpu.HBM)
            for operand in (
                lengths, hidden_in, frozen_query_rows, base_key_value, cache,
                old_down_q, current_query_up, old_down_o, old_up_o,
                new_down_q, refreshed_query_up, new_down_o, new_up_o,
            )
        ],
    )
    written = jax.ShapeDtypeStruct(frozen_query_rows.shape, BF16)
    return pl.pallas_call(
        write_out,
        out_shape=(written, written),
        in_specs=[pl.BlockSpec(memory_space=pltpu.VMEM)] * 2,
        out_specs=(pl.BlockSpec(memory_space=pl.ANY),) * 2,
        scratch_shapes=[dma((2,))],
    )(*[pltpu.with_memory_space_constraint(result, pltpu.VMEM) for result in results])


def solution(mesh):
    placed = (
        P(None, "replica", None),
        P(None, "replica", "tensor"),
        P(None, None, "replica", "tensor"),
        P(None, "replica", None, "tensor"),
        P("replica"),
        P("replica"),
        P(),
        P(None, "tensor"),
        P(None, "tensor"),
        P(),
        P("replica", None),
        P("replica", "tensor"),
        P("replica", "tensor"),
        P("replica", None),
    )
    return jax.shard_map(
        functools.partial(body, mesh.shape["replica"], mesh.shape["tensor"]),
        mesh=mesh,
        in_specs=placed,
        out_specs=(P(None, "replica", "tensor"), P(None, "replica", "tensor")),
        check_vma=False,
    )
```

```python
import functools

import jax
import jax.numpy as jnp
from jax import lax
from jax.experimental import pallas as pl
from jax.experimental.pallas import tpu as pltpu
from jax.sharding import PartitionSpec as P

HD = 128
STEPS = 3
ROWS = 8
RANK = 64
GROUP = 16
LANES = 128
HALF = ROWS // 2
SHARES = 4
MESH = pl.DeviceIdType.MESH
F32 = jnp.float32
BF16 = jnp.bfloat16


def nt(a, b):
    return lax.dot_general(a, b, (((1,), (1,)), ((), ())), preferred_element_type=F32)


def nn(a, b):
    return lax.dot_general(a, b, (((1,), (0,)), ((), ())), preferred_element_type=F32)


def kernel(
    n_block, n_tensor, width, cache_len, key_rows,
    switch, lengths_in, hidden, frozen, fresh, cache,
    old_dq, old_uq, old_do, old_uo, new_dq, new_uq, new_do, new_uo,
    attended_out, adapter_out,
    row_dq, row_uq, row_do, row_uo, hid_own, hid_rows, hid_full, dq_full, frz, frs, kbuf, vbuf,
    w_old, w_new, pack_q, landed_q, stage_q, spread_q, packs, landed, stage, spread, fresh_rows, old_rank, q_heads, a_rows,
    rank_part, rank_parts, part, parts, lengths,
    others_in, loc, kv_sem, q_send, q_recv, s1_send, s1_recv, hid_send, hid_recv, s2_send, s2_recv,
    rank_send, rank_recv, sum_send, sum_recv,
):
    replica = lax.axis_index("replica")
    tensor = lax.axis_index("tensor")
    mine = lax.rem(replica, GROUP)
    block = lax.div(replica, GROUP)
    base = block * GROUP
    cols = pl.ds(pl.multiple_of(tensor * width, width), width)
    leads = tensor < SHARES
    share_width = n_tensor // SHARES * width
    rank_cols = pl.ds(
        pl.multiple_of(lax.rem(tensor, SHARES) * share_width, share_width), share_width
    )
    rank_tiles = share_width // LANES
    heads = width // HD
    tiles = width // LANES

    def block_at(j):
        return lax.rem(block + j, n_block)

    def tensor_at(j):
        return lax.rem(tensor + j, n_tensor)

    block_order = sorted(range(n_block), key=lambda j: -min(j, n_block - j))
    tensor_order = sorted(range(n_tensor), key=lambda j: -min(j, n_tensor - j))
    group_peers = [
        (base + lax.rem(mine + GROUP // 2 + j, GROUP), tensor)
        for j in sorted(range(1 - GROUP // 2, GROUP // 2), key=abs)
    ]
    block_peers = [(block_at(j) * GROUP + mine, tensor) for j in block_order if j]
    tensor_peers = [(replica, tensor_at(j)) for j in tensor_order if j]
    rank_peers = [
        (block_at(i), (block_at(i) * GROUP + mine, tensor_at(j)))
        for i in block_order
        for j in tensor_order
        if i or j
    ]
    def send(src, dst, send_sem, recv_sem, peer):
        pltpu.make_async_remote_copy(
            src_ref=src,
            dst_ref=dst,
            send_sem=send_sem,
            recv_sem=recv_sem,
            device_id=peer,
            device_id_type=MESH,
        ).start()

    def wait_bytes(ref, sem):
        pltpu.make_async_copy(ref, ref, sem).wait()

    local = [
        pltpu.make_async_copy(new_dq, row_dq, loc.at[0]),
        pltpu.make_async_copy(new_uq, row_uq, loc.at[1]),
        pltpu.make_async_copy(new_do, row_do, loc.at[2]),
        pltpu.make_async_copy(new_uo, row_uo, loc.at[3]),
        pltpu.make_async_copy(hidden.at[:, :, rank_cols], hid_own.at[block], loc.at[4]),
        pltpu.make_async_copy(fresh, frs, loc.at[5]),
        pltpu.make_async_copy(hidden, hid_full, loc.at[6]),
        pltpu.make_async_copy(old_dq, dq_full, loc.at[7]),
        pltpu.make_async_copy(old_uq, w_old.at[0], loc.at[8]),
        pltpu.make_async_copy(frozen, frz, loc.at[9]),
        pltpu.make_async_copy(old_do, w_old.at[1], loc.at[10]),
        pltpu.make_async_copy(old_uo.at[:, cols], w_old.at[2], loc.at[11]),
        pltpu.make_async_copy(lengths_in, lengths, loc.at[12]),
    ]
    for copy in local[:5]:
        copy.start()
    barrier = pltpu.get_barrier_semaphore()
    own_half = lax.div(tensor, SHARES) * SHARES
    half_peers = [
        (replica, own_half + lax.rem(tensor + j, SHARES)) for j in range(1, SHARES)
    ]
    close = group_peers + block_peers + half_peers
    across = [
        (block_at(i) * GROUP + mine, SHARES - own_half + j)
        for i in block_order
        for j in range(SHARES)
    ]

    def signal(semaphore, peers):
        for peer in peers:
            pl.semaphore_signal(semaphore, inc=1, device_id=peer, device_id_type=MESH)

    signal(barrier, close)

    @pl.when(leads)
    def _():
        signal(barrier, across)

    kv = []
    for b in range(ROWS):
        kv.append(pltpu.make_async_copy(cache.at[0, b], kbuf.at[b, pl.ds(0, cache_len)], kv_sem.at[0, b]))
        kv.append(pltpu.make_async_copy(cache.at[1, b], vbuf.at[b, pl.ds(0, cache_len)], kv_sem.at[1, b]))

    def tiled(buf, rows):
        at = 0
        for row in rows:
            row = row.astype(F32)
            for c in range(row.shape[1] // LANES):
                buf[pl.ds(at + c, 1), :] = row[:, c * LANES : (c + 1) * LANES]
            at += row.shape[1] // LANES

    local[0].wait()

    @pl.when(leads)
    def _():
        tiled(stage_q, [row_dq[:, rank_cols]])
        pack_q[...] = stage_q[...].astype(BF16)
        landed_q[mine] = pack_q[...]

    @pl.when(leads)
    def _():
        pl.semaphore_wait(barrier, len(close))

    @pl.when(jnp.logical_not(leads))
    def _():
        pl.semaphore_wait(barrier, len(close) + len(across))
        signal(others_in, across)


    local[4].wait()

    @pl.when(leads)
    def _():
        for peer in block_peers:
            send(hid_own.at[block], hid_own.at[block], hid_send, hid_recv, peer)

    @pl.when(leads)
    def _():
        for peer in group_peers:
            send(pack_q, landed_q.at[mine], q_send, q_recv, peer)

    def spread_rows(p, rows):
        tiled(stage.at[p], rows)
        packs[p] = stage[p].astype(BF16)
        landed[p, mine] = packs[p]
        for peer in group_peers:
            send(packs.at[p], landed.at[p, mine], s1_send.at[p], s1_recv.at[p], peer)

    for copy in local[1:3]:
        copy.wait()
    spread_rows(0, [row_uq[...], row_do[...]])

    local[3].wait()
    spread_rows(1, [row_uo[:, cols], jnp.zeros((1, width), F32)])

    for copy in local[5:] + kv:
        copy.start()

    local[5].wait()
    pad = key_rows - cache_len - 16
    for i, buf in enumerate((kbuf, vbuf)):
        for u in range(ROWS):
            if u < STEPS:
                fresh_rows[i, pl.ds(u * ROWS, ROWS), :] = frs[i, u].astype(F32)
            else:
                fresh_rows[i, pl.ds(u * ROWS, ROWS), :] = jnp.zeros((ROWS, HD), F32)
        for b in range(ROWS):
            rows = fresh_rows[i, pl.ds(b, ROWS, stride=ROWS), :]
            rows = jnp.concatenate([rows, jnp.zeros((8, HD), F32)], axis=0)
            buf[b, pl.ds(cache_len, 16), :] = rows.astype(BF16)
            buf[b, pl.ds(cache_len + 16, pad), :] = jnp.zeros((pad, HD), BF16)

    local[6].wait()
    local[7].wait()
    old_rank[...] = jnp.zeros_like(old_rank)
    old = jnp.zeros((STEPS * ROWS, RANK), F32)
    for c in range(n_tensor):
        at = slice(c * width, (c + 1) * width)
        rows = jnp.concatenate([hid_full[t, :, at].astype(F32) for t in range(STEPS)], axis=0)
        old = old + nt(rows.astype(BF16), dq_full[:, at])
    old_rank[:, 0:RANK] = old

    own_rows = pl.ds(pl.multiple_of(block * GROUP, GROUP), GROUP)
    lane = lax.broadcasted_iota(jnp.int32, (ROWS, LANES), 1)
    lane_half = lax.div(lane, RANK)
    lane_group = lax.div(lane, GROUP)

    def arrived(p):
        wait_bytes(landed.at[p, pl.ds(0, GROUP - 1)], s1_recv.at[p])
        spread[p] = landed[p].reshape(GROUP * 2 * tiles, LANES).astype(F32)

    def rows_of(i):
        return [
            spread[i // 2, pl.ds((i % 2) * tiles + s, GROUP, stride=2 * tiles), :].astype(BF16)
            for s in range(tiles)
        ]

    def share(m):
        for s, tile in enumerate(rows_of(m)):
            w_new[m, own_rows, s * LANES : (s + 1) * LANES] = tile
        for peer in block_peers:
            send(w_new.at[m, own_rows], w_new.at[m, own_rows], s2_send.at[m], s2_recv.at[m], peer)

    def weights(m):
        wait_bytes(w_new.at[m, pl.ds(0, (n_block - 1) * GROUP)], s2_recv.at[m])
        return jnp.concatenate([w_old[m], w_new[m]], axis=0)

    @pl.when(leads)
    def _():
        wait_bytes(hid_own.at[pl.ds(0, n_block - 1)], hid_recv)
        for k in range(n_block):
            rows = jnp.concatenate([hid_own[k, t].astype(F32) for t in range(STEPS)], axis=0)
            hid_rows[pl.ds(k * STEPS * ROWS, STEPS * ROWS), :] = rows.astype(BF16)
        wait_bytes(landed_q.at[pl.ds(0, GROUP - 1)], q_recv)
        spread_q[...] = landed_q[...].reshape(GROUP * rank_tiles, LANES).astype(F32)
        down_q = jnp.concatenate(
            [
                spread_q[pl.ds(c, GROUP, stride=rank_tiles), :].astype(BF16)
                for c in range(rank_tiles)
            ],
            axis=1,
        )
        ranks = nt(hid_rows[...], jnp.concatenate([down_q] * (LANES // GROUP), axis=0))
        for k in range(n_block):
            tile = jnp.zeros((ROWS, LANES), F32)
            for t in range(STEPS):
                at = (k * STEPS + t) * ROWS
                tile = jnp.where(lane_group == t, ranks[at : at + ROWS], tile)
            rank_part[k] = tile[:HALF] + pltpu.roll(tile[HALF:], STEPS * GROUP, 1)
        slot = block * SHARES + tensor
        rank_parts[slot] = rank_part[block]
        pl.semaphore_wait(others_in, len(across))
        for k, peer in rank_peers:
            send(rank_part.at[k], rank_parts.at[slot], rank_send, rank_recv, peer)

    arrived(0)
    share(0)
    share(1)
    arrived(1)
    share(2)

    switch_at = jnp.full((ROWS, LANES), switch[0], jnp.int32)
    half_of = [jnp.where(switch_at <= t, 1, 0) for t in range(STEPS)]

    for i in (8, 9, 10, 11, 12):
        local[i].wait()
    for copy in kv:
        copy.wait()

    @pl.when(leads)
    def _():
        wait_bytes(rank_parts.at[pl.ds(0, n_block * SHARES - 1)], rank_recv)

    @pl.when(jnp.logical_not(leads))
    def _():
        wait_bytes(rank_parts.at[pl.ds(0, n_block * SHARES)], rank_recv)

    sums = []
    for k in range(n_block):
        tile = jnp.sum(rank_parts[k * SHARES : (k + 1) * SHARES], axis=0)
        sums.append(
            jnp.concatenate([tile, pltpu.roll(tile, LANES - STEPS * GROUP, 1)], axis=0)
        )
    chosen = []
    for t in range(STEPS):
        both = old_rank[t * ROWS : (t + 1) * ROWS]
        for k in range(n_block):
            at = RANK // GROUP + k
            moved = pltpu.roll(sums[k], (at - t) * GROUP, 1)
            both = jnp.where(lane_group == at, moved, both)
        chosen.append(jnp.where(lane_half == half_of[t], both, 0.0))
    low_rank = jnp.concatenate(chosen, axis=0).astype(BF16)
    delta = nn(low_rank, weights(0))
    for t in range(STEPS):
        for h in range(heads):
            at = slice(h * HD, (h + 1) * HD)
            q_heads[t, pl.ds(h * ROWS, ROWS), :] = (
                frz[t, :, at].astype(F32) + delta[t * ROWS : (t + 1) * ROWS, at]
            )

    scale = 1.0 / HD**0.5
    query_rows = STEPS * heads
    col = lax.broadcasted_iota(jnp.int32, (query_rows, key_rows), 1)
    row = lax.broadcasted_iota(jnp.int32, (query_rows, key_rows), 0)
    is_fresh = jnp.logical_and(col >= cache_len, (col - cache_len) * heads <= row)
    queries = [
        jnp.concatenate([q_heads[t, pl.ds(b, heads, stride=ROWS), :] for t in range(STEPS)], axis=0).astype(BF16)
        for b in range(ROWS)
    ]
    scores = [nt(queries[b], kbuf[b]) for b in range(ROWS)]
    probs = []
    for b in range(ROWS):
        live = jnp.logical_or(col < lengths[b], is_fresh)
        shown = jnp.where(live, scores[b] * scale, -1e30)
        top = jnp.max(shown, axis=1, keepdims=True)
        exps = jnp.exp(shown - top)
        total = jnp.sum(exps, axis=1, keepdims=True)
        probs.append((exps * (1.0 / total)).astype(BF16))
    for b in range(ROWS):
        result = nn(probs[b], vbuf[b])
        for t in range(STEPS):
            a_rows[t, pl.ds(b * heads, heads), :] = result[t * heads : (t + 1) * heads]

    attended = []
    for t in range(STEPS):
        rows = jnp.concatenate(
            [a_rows[t, pl.ds(h, ROWS, stride=heads), :] for h in range(heads)], axis=1
        )
        attended.append(rows)
        attended_out[t] = rows.astype(BF16)

    product = nt(jnp.concatenate(attended, axis=0).astype(BF16), weights(1))
    picked = []
    for t in range(STEPS):
        rows = product[t * ROWS : (t + 1) * ROWS]
        picked.append(jnp.where(half_of[t] == t % 2, rows, pltpu.roll(rows, RANK, 1)))
    tile = jnp.where(lane_half == 0, picked[0], picked[1])
    last = jnp.where(
        lane_half[:HALF] == 0, picked[2][:HALF], pltpu.roll(picked[2][HALF:], RANK, 1)
    )
    for i, piece in enumerate((tile[:HALF], tile[HALF:], last)):
        part[i] = piece
        parts[tensor, i] = piece
    for peer in tensor_peers:
        send(part, parts.at[tensor], sum_send, sum_recv, peer)

    up_o = weights(2)
    wait_bytes(parts.at[pl.ds(0, n_tensor - 1)], sum_recv)
    total = jnp.sum(parts[...], axis=0)
    tile = jnp.concatenate([total[0], total[1]], axis=0)
    other = pltpu.roll(tile, RANK, 1)
    last = jnp.concatenate([total[2], total[2]], axis=0)
    last_other = pltpu.roll(last, RANK, 1)
    row_half = lax.div(lax.broadcasted_iota(jnp.int32, (ROWS, LANES), 0), HALF)
    both = (
        jnp.where(lane_half == 0, tile, other),
        jnp.where(lane_half == 1, tile, other),
        jnp.where(lane_half == row_half, last, last_other),
    )
    rows = [jnp.where(lane_half == half_of[t], both[t], 0.0) for t in range(STEPS)]
    result = nn(jnp.concatenate(rows, axis=0).astype(BF16), up_o)
    for t in range(STEPS):
        adapter_out[t] = result[t * ROWS : (t + 1) * ROWS].astype(BF16)

    for p in range(2):
        wait_bytes(landed.at[p, pl.ds(0, GROUP - 1)], s1_send.at[p])
    for m in range(3):
        wait_bytes(w_new.at[m, pl.ds(0, (n_block - 1) * GROUP)], s2_send.at[m])

    @pl.when(leads)
    def _():
        wait_bytes(landed_q.at[pl.ds(0, GROUP - 1)], q_send)
        wait_bytes(hid_own.at[pl.ds(0, n_block - 1)], hid_send)
        wait_bytes(rank_parts.at[pl.ds(0, n_block * SHARES)], rank_send)
        wait_bytes(rank_parts.at[pl.ds(0, n_block * SHARES - 1)], rank_send)

    wait_bytes(parts.at[pl.ds(0, n_tensor - 1)], sum_send)


def write_out(attended, adapter, attended_out, adapter_out, sems):
    copies = [
        pltpu.make_async_copy(attended, attended_out, sems.at[0]),
        pltpu.make_async_copy(adapter, adapter_out, sems.at[1]),
    ]
    for copy in copies:
        copy.start()
    for copy in copies:
        copy.wait()


def body(
    n_replica, n_tensor,
    hidden_in, frozen_query_rows, base_key_value, cache, lengths, switch_step,
    old_down_q, current_query_up, old_down_o, old_up_o,
    new_down_q, refreshed_query_up, new_down_o, new_up_o,
):
    width = frozen_query_rows.shape[-1]
    cache_len = cache.shape[2]
    key_rows = cache_len + LANES
    tiles = width // LANES
    n_block = n_replica // GROUP
    share_width = n_tensor // SHARES * width
    rank_tiles = share_width // LANES
    dma = pltpu.SemaphoreType.DMA
    out = pltpu.VMEM(frozen_query_rows.shape, BF16)
    results = pl.pallas_call(
        functools.partial(kernel, n_block, n_tensor, width, cache_len, key_rows),
        out_shape=(out, out),
        in_specs=[pl.BlockSpec(memory_space=pltpu.SMEM)]
        + [pl.BlockSpec(memory_space=pltpu.HBM)] * 13,
        out_specs=(pl.BlockSpec(memory_space=pltpu.VMEM),) * 2,
        scratch_shapes=[
            pltpu.VMEM(new_down_q.shape, BF16),
            pltpu.VMEM(refreshed_query_up.shape, BF16),
            pltpu.VMEM(new_down_o.shape, BF16),
            pltpu.VMEM(new_up_o.shape, BF16),
            pltpu.VMEM((n_block, STEPS, ROWS, share_width), BF16),
            pltpu.VMEM((n_block * STEPS * ROWS, share_width), BF16),
            pltpu.VMEM(hidden_in.shape, BF16),
            pltpu.VMEM(old_down_q.shape, BF16),
            pltpu.VMEM((STEPS, ROWS, width), BF16),
            pltpu.VMEM(base_key_value.shape, BF16),
            pltpu.VMEM((ROWS, key_rows, HD), BF16),
            pltpu.VMEM((ROWS, key_rows, HD), BF16),
            pltpu.VMEM((3, RANK, width), BF16),
            pltpu.VMEM((3, RANK, width), BF16),
            pltpu.VMEM((rank_tiles, LANES), BF16),
            pltpu.VMEM((GROUP, rank_tiles, LANES), BF16),
            pltpu.VMEM((rank_tiles, LANES), F32),
            pltpu.VMEM((GROUP * rank_tiles, LANES), F32),
            pltpu.VMEM((2, 2 * tiles, LANES), BF16),
            pltpu.VMEM((2, GROUP, 2 * tiles, LANES), BF16),
            pltpu.VMEM((2, 2 * tiles, LANES), F32),
            pltpu.VMEM((2, GROUP * 2 * tiles, LANES), F32),
            pltpu.VMEM((2, ROWS * ROWS, HD), F32),
            pltpu.VMEM((STEPS * ROWS, LANES), F32),
            pltpu.VMEM((STEPS, width // HD * ROWS, HD), F32),
            pltpu.VMEM((STEPS, width // HD * ROWS, HD), F32),
            pltpu.VMEM((n_block, HALF, LANES), F32),
            pltpu.VMEM((n_block * SHARES, HALF, LANES), F32),
            pltpu.VMEM((STEPS, HALF, LANES), F32),
            pltpu.VMEM((n_tensor, STEPS, HALF, LANES), F32),
            pltpu.SMEM(lengths.shape, jnp.int32),
            pltpu.SemaphoreType.REGULAR,
            dma((13,)),
            dma((2, ROWS)),
            dma(()),
            dma(()),
            dma((2,)),
            dma((2,)),
            dma(()),
            dma(()),
            dma((3,)),
            dma((3,)),
            dma(()),
            dma(()),
            dma(()),
            dma(()),
        ],
        compiler_params=pltpu.CompilerParams(
            collective_id=0, has_side_effects=True, vmem_limit_bytes=32 * 1024 * 1024
        ),
    )(
        switch_step,
        *[
            pltpu.with_memory_space_constraint(operand, pltpu.HBM)
            for operand in (
                lengths, hidden_in, frozen_query_rows, base_key_value, cache,
                old_down_q, current_query_up, old_down_o, old_up_o,
                new_down_q, refreshed_query_up, new_down_o, new_up_o,
            )
        ],
    )
    written = jax.ShapeDtypeStruct(frozen_query_rows.shape, BF16)
    return pl.pallas_call(
        write_out,
        out_shape=(written, written),
        in_specs=[pl.BlockSpec(memory_space=pltpu.VMEM)] * 2,
        out_specs=(pl.BlockSpec(memory_space=pl.ANY),) * 2,
        scratch_shapes=[dma((2,))],
    )(*[pltpu.with_memory_space_constraint(result, pltpu.VMEM) for result in results])


def solution(mesh):
    placed = (
        P(None, "replica", None),
        P(None, "replica", "tensor"),
        P(None, None, "replica", "tensor"),
        P(None, "replica", None, "tensor"),
        P("replica"),
        P("replica"),
        P(),
        P(None, "tensor"),
        P(None, "tensor"),
        P(),
        P("replica", None),
        P("replica", "tensor"),
        P("replica", "tensor"),
        P("replica", None),
    )
    return jax.shard_map(
        functools.partial(body, mesh.shape["replica"], mesh.shape["tensor"]),
        mesh=mesh,
        in_specs=placed,
        out_specs=(P(None, "replica", "tensor"), P(None, "replica", "tensor")),
        check_vma=False,
    )
```

```python
import functools

import jax
import jax.numpy as jnp
from jax import lax
from jax.experimental import pallas as pl
from jax.experimental.pallas import tpu as pltpu
from jax.sharding import PartitionSpec as P

HD = 128
STEPS = 3
ROWS = 8
RANK = 64
GROUP = 16
LANES = 128
HALF = ROWS // 2
SHARES = 4
MESH = pl.DeviceIdType.MESH
F32 = jnp.float32
BF16 = jnp.bfloat16


def nt(a, b):
    return lax.dot_general(a, b, (((1,), (1,)), ((), ())), preferred_element_type=F32)


def nn(a, b):
    return lax.dot_general(a, b, (((1,), (0,)), ((), ())), preferred_element_type=F32)


def kernel(
    n_block, n_tensor, width, cache_len, key_rows,
    switch, lengths_in, hidden, frozen, fresh, cache,
    old_dq, old_uq, old_do, old_uo, new_dq, new_uq, new_do, new_uo,
    attended_out, adapter_out,
    row_dq, row_uq, row_do, row_uo, hid_own, hid_rows, hid_full, dq_full, frz, frs, kbuf, vbuf,
    w_old, w_new, pack_q, landed_q, stage_q, spread_q, packs, landed, stage, spread, fresh_rows, old_rank, q_heads, a_rows,
    rank_part, rank_parts, part, parts, lengths,
    others_in, loc, kv_sem, q_send, q_recv, s1_send, s1_recv, hid_send, hid_recv, s2_send, s2_recv,
    rank_send, rank_recv, sum_send, sum_recv,
):
    replica = lax.axis_index("replica")
    tensor = lax.axis_index("tensor")
    mine = lax.rem(replica, GROUP)
    block = lax.div(replica, GROUP)
    base = block * GROUP
    cols = pl.ds(pl.multiple_of(tensor * width, width), width)
    leads = tensor < SHARES
    share_width = n_tensor // SHARES * width
    rank_cols = pl.ds(
        pl.multiple_of(lax.rem(tensor, SHARES) * share_width, share_width), share_width
    )
    rank_tiles = share_width // LANES
    heads = width // HD
    tiles = width // LANES

    def block_at(j):
        return lax.rem(block + j, n_block)

    def tensor_at(j):
        return lax.rem(tensor + j, n_tensor)

    block_order = sorted(range(n_block), key=lambda j: -min(j, n_block - j))
    tensor_order = sorted(range(n_tensor), key=lambda j: -min(j, n_tensor - j))
    group_peers = [
        (base + lax.rem(mine + GROUP // 2 + j, GROUP), tensor)
        for j in sorted(range(1 - GROUP // 2, GROUP // 2), key=abs)
    ]
    block_peers = [(block_at(j) * GROUP + mine, tensor) for j in block_order if j]
    tensor_peers = [(replica, tensor_at(j)) for j in tensor_order if j]
    rank_peers = [
        (block_at(i), (block_at(i) * GROUP + mine, tensor_at(j)))
        for i in block_order
        for j in tensor_order
        if i or j
    ]
    def send(src, dst, send_sem, recv_sem, peer):
        pltpu.make_async_remote_copy(
            src_ref=src,
            dst_ref=dst,
            send_sem=send_sem,
            recv_sem=recv_sem,
            device_id=peer,
            device_id_type=MESH,
        ).start()

    def wait_bytes(ref, sem):
        pltpu.make_async_copy(ref, ref, sem).wait()

    local = [
        pltpu.make_async_copy(new_dq, row_dq, loc.at[0]),
        pltpu.make_async_copy(new_uq, row_uq, loc.at[1]),
        pltpu.make_async_copy(new_do, row_do, loc.at[2]),
        pltpu.make_async_copy(new_uo, row_uo, loc.at[3]),
        pltpu.make_async_copy(hidden.at[:, :, rank_cols], hid_own.at[block], loc.at[4]),
        pltpu.make_async_copy(fresh, frs, loc.at[5]),
        pltpu.make_async_copy(hidden, hid_full, loc.at[6]),
        pltpu.make_async_copy(old_dq, dq_full, loc.at[7]),
        pltpu.make_async_copy(old_uq, w_old.at[0], loc.at[8]),
        pltpu.make_async_copy(frozen, frz, loc.at[9]),
        pltpu.make_async_copy(old_do, w_old.at[1], loc.at[10]),
        pltpu.make_async_copy(old_uo.at[:, cols], w_old.at[2], loc.at[11]),
        pltpu.make_async_copy(lengths_in, lengths, loc.at[12]),
    ]
    for copy in local[1:4]:
        copy.start()

    @pl.when(leads)
    def _():
        local[0].start()
        local[4].start()

    barrier = pltpu.get_barrier_semaphore()
    own_half = lax.div(tensor, SHARES) * SHARES
    half_peers = [
        (replica, own_half + lax.rem(tensor + j, SHARES)) for j in range(1, SHARES)
    ]
    close = group_peers + block_peers + half_peers
    across = [
        (block_at(i) * GROUP + mine, SHARES - own_half + j)
        for i in block_order
        for j in range(SHARES)
    ]

    def signal(semaphore, peers):
        for peer in peers:
            pl.semaphore_signal(semaphore, inc=1, device_id=peer, device_id_type=MESH)

    signal(barrier, close)

    @pl.when(leads)
    def _():
        signal(barrier, across)

    kv = []
    for b in range(ROWS):
        kv.append(pltpu.make_async_copy(cache.at[0, b], kbuf.at[b, pl.ds(0, cache_len)], kv_sem.at[0, b]))
        kv.append(pltpu.make_async_copy(cache.at[1, b], vbuf.at[b, pl.ds(0, cache_len)], kv_sem.at[1, b]))

    def tiled(buf, rows):
        at = 0
        for row in rows:
            row = row.astype(F32)
            for c in range(row.shape[1] // LANES):
                buf[pl.ds(at + c, 1), :] = row[:, c * LANES : (c + 1) * LANES]
            at += row.shape[1] // LANES

    @pl.when(leads)
    def _():
        local[0].wait()
        tiled(stage_q, [row_dq[:, rank_cols]])
        pack_q[...] = stage_q[...].astype(BF16)
        landed_q[mine] = pack_q[...]

    @pl.when(leads)
    def _():
        pl.semaphore_wait(barrier, len(close))

    @pl.when(jnp.logical_not(leads))
    def _():
        pl.semaphore_wait(barrier, len(close) + len(across))
        signal(others_in, across)


    @pl.when(leads)
    def _():
        local[4].wait()
        for peer in block_peers:
            send(hid_own.at[block], hid_own.at[block], hid_send, hid_recv, peer)

    @pl.when(leads)
    def _():
        for peer in group_peers:
            send(pack_q, landed_q.at[mine], q_send, q_recv, peer)

    def spread_rows(p, rows):
        tiled(stage.at[p], rows)
        packs[p] = stage[p].astype(BF16)
        landed[p, mine] = packs[p]
        for peer in group_peers:
            send(packs.at[p], landed.at[p, mine], s1_send.at[p], s1_recv.at[p], peer)

    for copy in local[1:3]:
        copy.wait()
    spread_rows(0, [row_uq[...], row_do[...]])

    local[3].wait()
    spread_rows(1, [row_uo[:, cols], jnp.zeros((1, width), F32)])

    for copy in local[5:] + kv:
        copy.start()

    local[5].wait()
    pad = key_rows - cache_len - 16
    for i, buf in enumerate((kbuf, vbuf)):
        for u in range(ROWS):
            if u < STEPS:
                fresh_rows[i, pl.ds(u * ROWS, ROWS), :] = frs[i, u].astype(F32)
            else:
                fresh_rows[i, pl.ds(u * ROWS, ROWS), :] = jnp.zeros((ROWS, HD), F32)
        for b in range(ROWS):
            rows = fresh_rows[i, pl.ds(b, ROWS, stride=ROWS), :]
            rows = jnp.concatenate([rows, jnp.zeros((8, HD), F32)], axis=0)
            buf[b, pl.ds(cache_len, 16), :] = rows.astype(BF16)
            buf[b, pl.ds(cache_len + 16, pad), :] = jnp.zeros((pad, HD), BF16)

    local[6].wait()
    local[7].wait()
    old_rank[...] = jnp.zeros_like(old_rank)
    old = jnp.zeros((STEPS * ROWS, RANK), F32)
    for c in range(n_tensor):
        at = slice(c * width, (c + 1) * width)
        rows = jnp.concatenate([hid_full[t, :, at].astype(F32) for t in range(STEPS)], axis=0)
        old = old + nt(rows.astype(BF16), dq_full[:, at])
    old_rank[:, 0:RANK] = old

    own_rows = pl.ds(pl.multiple_of(block * GROUP, GROUP), GROUP)
    lane = lax.broadcasted_iota(jnp.int32, (ROWS, LANES), 1)
    lane_half = lax.div(lane, RANK)
    lane_group = lax.div(lane, GROUP)

    def arrived(p):
        wait_bytes(landed.at[p, pl.ds(0, GROUP - 1)], s1_recv.at[p])
        spread[p] = landed[p].reshape(GROUP * 2 * tiles, LANES).astype(F32)

    def rows_of(i):
        return [
            spread[i // 2, pl.ds((i % 2) * tiles + s, GROUP, stride=2 * tiles), :].astype(BF16)
            for s in range(tiles)
        ]

    def share(m):
        for s, tile in enumerate(rows_of(m)):
            w_new[m, own_rows, s * LANES : (s + 1) * LANES] = tile
        for peer in block_peers:
            send(w_new.at[m, own_rows], w_new.at[m, own_rows], s2_send.at[m], s2_recv.at[m], peer)

    def weights(m):
        wait_bytes(w_new.at[m, pl.ds(0, (n_block - 1) * GROUP)], s2_recv.at[m])
        return jnp.concatenate([w_old[m], w_new[m]], axis=0)

    @pl.when(leads)
    def _():
        wait_bytes(hid_own.at[pl.ds(0, n_block - 1)], hid_recv)
        for k in range(n_block):
            rows = jnp.concatenate([hid_own[k, t].astype(F32) for t in range(STEPS)], axis=0)
            hid_rows[pl.ds(k * STEPS * ROWS, STEPS * ROWS), :] = rows.astype(BF16)
        wait_bytes(landed_q.at[pl.ds(0, GROUP - 1)], q_recv)
        spread_q[...] = landed_q[...].reshape(GROUP * rank_tiles, LANES).astype(F32)
        down_q = jnp.concatenate(
            [
                spread_q[pl.ds(c, GROUP, stride=rank_tiles), :].astype(BF16)
                for c in range(rank_tiles)
            ],
            axis=1,
        )
        ranks = nt(hid_rows[...], jnp.concatenate([down_q] * (LANES // GROUP), axis=0))
        for k in range(n_block):
            tile = jnp.zeros((ROWS, LANES), F32)
            for t in range(STEPS):
                at = (k * STEPS + t) * ROWS
                tile = jnp.where(lane_group == t, ranks[at : at + ROWS], tile)
            rank_part[k] = tile[:HALF] + pltpu.roll(tile[HALF:], STEPS * GROUP, 1)
        slot = block * SHARES + tensor
        rank_parts[slot] = rank_part[block]
        pl.semaphore_wait(others_in, len(across))
        for k, peer in rank_peers:
            send(rank_part.at[k], rank_parts.at[slot], rank_send, rank_recv, peer)

    arrived(0)
    share(1)
    share(0)
    arrived(1)
    share(2)

    switch_at = jnp.full((ROWS, LANES), switch[0], jnp.int32)
    half_of = [jnp.where(switch_at <= t, 1, 0) for t in range(STEPS)]

    for i in (8, 9, 10, 11, 12):
        local[i].wait()
    for copy in kv:
        copy.wait()

    @pl.when(leads)
    def _():
        wait_bytes(rank_parts.at[pl.ds(0, n_block * SHARES - 1)], rank_recv)

    @pl.when(jnp.logical_not(leads))
    def _():
        wait_bytes(rank_parts.at[pl.ds(0, n_block * SHARES)], rank_recv)

    sums = []
    for k in range(n_block):
        tile = jnp.sum(rank_parts[k * SHARES : (k + 1) * SHARES], axis=0)
        sums.append(
            jnp.concatenate([tile, pltpu.roll(tile, LANES - STEPS * GROUP, 1)], axis=0)
        )
    chosen = []
    for t in range(STEPS):
        both = old_rank[t * ROWS : (t + 1) * ROWS]
        for k in range(n_block):
            at = RANK // GROUP + k
            moved = pltpu.roll(sums[k], (at - t) * GROUP, 1)
            both = jnp.where(lane_group == at, moved, both)
        chosen.append(jnp.where(lane_half == half_of[t], both, 0.0))
    low_rank = jnp.concatenate(chosen, axis=0).astype(BF16)
    delta = nn(low_rank, weights(0))
    for t in range(STEPS):
        for h in range(heads):
            at = slice(h * HD, (h + 1) * HD)
            q_heads[t, pl.ds(h * ROWS, ROWS), :] = (
                frz[t, :, at].astype(F32) + delta[t * ROWS : (t + 1) * ROWS, at]
            )

    scale = 1.0 / HD**0.5
    query_rows = STEPS * heads
    col = lax.broadcasted_iota(jnp.int32, (query_rows, key_rows), 1)
    row = lax.broadcasted_iota(jnp.int32, (query_rows, key_rows), 0)
    is_fresh = jnp.logical_and(col >= cache_len, (col - cache_len) * heads <= row)
    queries = [
        jnp.concatenate([q_heads[t, pl.ds(b, heads, stride=ROWS), :] for t in range(STEPS)], axis=0).astype(BF16)
        for b in range(ROWS)
    ]
    scores = [nt(queries[b], kbuf[b]) for b in range(ROWS)]
    probs = []
    for b in range(ROWS):
        live = jnp.logical_or(col < lengths[b], is_fresh)
        shown = jnp.where(live, scores[b] * scale, -1e30)
        top = jnp.max(shown, axis=1, keepdims=True)
        exps = jnp.exp(shown - top)
        total = jnp.sum(exps, axis=1, keepdims=True)
        probs.append((exps * (1.0 / total)).astype(BF16))
    for b in range(ROWS):
        result = nn(probs[b], vbuf[b])
        for t in range(STEPS):
            a_rows[t, pl.ds(b * heads, heads), :] = result[t * heads : (t + 1) * heads]

    attended = []
    for t in range(STEPS):
        rows = jnp.concatenate(
            [a_rows[t, pl.ds(h, ROWS, stride=heads), :] for h in range(heads)], axis=1
        )
        attended.append(rows)
        attended_out[t] = rows.astype(BF16)

    product = nt(jnp.concatenate(attended, axis=0).astype(BF16), weights(1))
    picked = []
    for t in range(STEPS):
        rows = product[t * ROWS : (t + 1) * ROWS]
        picked.append(jnp.where(half_of[t] == t % 2, rows, pltpu.roll(rows, RANK, 1)))
    tile = jnp.where(lane_half == 0, picked[0], picked[1])
    last = jnp.where(
        lane_half[:HALF] == 0, picked[2][:HALF], pltpu.roll(picked[2][HALF:], RANK, 1)
    )
    for i, piece in enumerate((tile[:HALF], tile[HALF:], last)):
        part[i] = piece
        parts[tensor, i] = piece
    for peer in tensor_peers:
        send(part, parts.at[tensor], sum_send, sum_recv, peer)

    up_o = weights(2)
    wait_bytes(parts.at[pl.ds(0, n_tensor - 1)], sum_recv)
    total = jnp.sum(parts[...], axis=0)
    tile = jnp.concatenate([total[0], total[1]], axis=0)
    other = pltpu.roll(tile, RANK, 1)
    last = jnp.concatenate([total[2], total[2]], axis=0)
    last_other = pltpu.roll(last, RANK, 1)
    row_half = lax.div(lax.broadcasted_iota(jnp.int32, (ROWS, LANES), 0), HALF)
    both = (
        jnp.where(lane_half == 0, tile, other),
        jnp.where(lane_half == 1, tile, other),
        jnp.where(lane_half == row_half, last, last_other),
    )
    rows = [jnp.where(lane_half == half_of[t], both[t], 0.0) for t in range(STEPS)]
    result = nn(jnp.concatenate(rows, axis=0).astype(BF16), up_o)
    for t in range(STEPS):
        adapter_out[t] = result[t * ROWS : (t + 1) * ROWS].astype(BF16)

    for p in range(2):
        wait_bytes(landed.at[p, pl.ds(0, GROUP - 1)], s1_send.at[p])
    for m in range(3):
        wait_bytes(w_new.at[m, pl.ds(0, (n_block - 1) * GROUP)], s2_send.at[m])

    @pl.when(leads)
    def _():
        wait_bytes(landed_q.at[pl.ds(0, GROUP - 1)], q_send)
        wait_bytes(hid_own.at[pl.ds(0, n_block - 1)], hid_send)
        wait_bytes(rank_parts.at[pl.ds(0, n_block * SHARES)], rank_send)
        wait_bytes(rank_parts.at[pl.ds(0, n_block * SHARES - 1)], rank_send)

    wait_bytes(parts.at[pl.ds(0, n_tensor - 1)], sum_send)


def write_out(attended, adapter, attended_out, adapter_out, sems):
    copies = [
        pltpu.make_async_copy(attended, attended_out, sems.at[0]),
        pltpu.make_async_copy(adapter, adapter_out, sems.at[1]),
    ]
    for copy in copies:
        copy.start()
    for copy in copies:
        copy.wait()


def body(
    n_replica, n_tensor,
    hidden_in, frozen_query_rows, base_key_value, cache, lengths, switch_step,
    old_down_q, current_query_up, old_down_o, old_up_o,
    new_down_q, refreshed_query_up, new_down_o, new_up_o,
):
    width = frozen_query_rows.shape[-1]
    cache_len = cache.shape[2]
    key_rows = cache_len + LANES
    tiles = width // LANES
    n_block = n_replica // GROUP
    share_width = n_tensor // SHARES * width
    rank_tiles = share_width // LANES
    dma = pltpu.SemaphoreType.DMA
    out = pltpu.VMEM(frozen_query_rows.shape, BF16)
    results = pl.pallas_call(
        functools.partial(kernel, n_block, n_tensor, width, cache_len, key_rows),
        out_shape=(out, out),
        in_specs=[pl.BlockSpec(memory_space=pltpu.SMEM)]
        + [pl.BlockSpec(memory_space=pltpu.HBM)] * 13,
        out_specs=(pl.BlockSpec(memory_space=pltpu.VMEM),) * 2,
        scratch_shapes=[
            pltpu.VMEM(new_down_q.shape, BF16),
            pltpu.VMEM(refreshed_query_up.shape, BF16),
            pltpu.VMEM(new_down_o.shape, BF16),
            pltpu.VMEM(new_up_o.shape, BF16),
            pltpu.VMEM((n_block, STEPS, ROWS, share_width), BF16),
            pltpu.VMEM((n_block * STEPS * ROWS, share_width), BF16),
            pltpu.VMEM(hidden_in.shape, BF16),
            pltpu.VMEM(old_down_q.shape, BF16),
            pltpu.VMEM((STEPS, ROWS, width), BF16),
            pltpu.VMEM(base_key_value.shape, BF16),
            pltpu.VMEM((ROWS, key_rows, HD), BF16),
            pltpu.VMEM((ROWS, key_rows, HD), BF16),
            pltpu.VMEM((3, RANK, width), BF16),
            pltpu.VMEM((3, RANK, width), BF16),
            pltpu.VMEM((rank_tiles, LANES), BF16),
            pltpu.VMEM((GROUP, rank_tiles, LANES), BF16),
            pltpu.VMEM((rank_tiles, LANES), F32),
            pltpu.VMEM((GROUP * rank_tiles, LANES), F32),
            pltpu.VMEM((2, 2 * tiles, LANES), BF16),
            pltpu.VMEM((2, GROUP, 2 * tiles, LANES), BF16),
            pltpu.VMEM((2, 2 * tiles, LANES), F32),
            pltpu.VMEM((2, GROUP * 2 * tiles, LANES), F32),
            pltpu.VMEM((2, ROWS * ROWS, HD), F32),
            pltpu.VMEM((STEPS * ROWS, LANES), F32),
            pltpu.VMEM((STEPS, width // HD * ROWS, HD), F32),
            pltpu.VMEM((STEPS, width // HD * ROWS, HD), F32),
            pltpu.VMEM((n_block, HALF, LANES), F32),
            pltpu.VMEM((n_block * SHARES, HALF, LANES), F32),
            pltpu.VMEM((STEPS, HALF, LANES), F32),
            pltpu.VMEM((n_tensor, STEPS, HALF, LANES), F32),
            pltpu.SMEM(lengths.shape, jnp.int32),
            pltpu.SemaphoreType.REGULAR,
            dma((13,)),
            dma((2, ROWS)),
            dma(()),
            dma(()),
            dma((2,)),
            dma((2,)),
            dma(()),
            dma(()),
            dma((3,)),
            dma((3,)),
            dma(()),
            dma(()),
            dma(()),
            dma(()),
        ],
        compiler_params=pltpu.CompilerParams(
            collective_id=0, has_side_effects=True, vmem_limit_bytes=32 * 1024 * 1024
        ),
    )(
        switch_step,
        *[
            pltpu.with_memory_space_constraint(operand, pltpu.HBM)
            for operand in (
                lengths, hidden_in, frozen_query_rows, base_key_value, cache,
                old_down_q, current_query_up, old_down_o, old_up_o,
                new_down_q, refreshed_query_up, new_down_o, new_up_o,
            )
        ],
    )
    written = jax.ShapeDtypeStruct(frozen_query_rows.shape, BF16)
    return pl.pallas_call(
        write_out,
        out_shape=(written, written),
        in_specs=[pl.BlockSpec(memory_space=pltpu.VMEM)] * 2,
        out_specs=(pl.BlockSpec(memory_space=pl.ANY),) * 2,
        scratch_shapes=[dma((2,))],
    )(*[pltpu.with_memory_space_constraint(result, pltpu.VMEM) for result in results])


def solution(mesh):
    placed = (
        P(None, "replica", None),
        P(None, "replica", "tensor"),
        P(None, None, "replica", "tensor"),
        P(None, "replica", None, "tensor"),
        P("replica"),
        P("replica"),
        P(),
        P(None, "tensor"),
        P(None, "tensor"),
        P(),
        P("replica", None),
        P("replica", "tensor"),
        P("replica", "tensor"),
        P("replica", None),
    )
    return jax.shard_map(
        functools.partial(body, mesh.shape["replica"], mesh.shape["tensor"]),
        mesh=mesh,
        in_specs=placed,
        out_specs=(P(None, "replica", "tensor"), P(None, "replica", "tensor")),
        check_vma=False,
    )
```
